128 devices in a mesh: chan: 4 (over y), feed: 32 (over z, x, core).
Axes of the slice: x: 4, y: 4, z: 4, core: 2. Of those that a mesh axis runs over, the one named last changes fastest.
Arguments:
- volt: bfloat16 [2, 1024, 32, 4096], P(None, 'feed', 'chan'), may hold values from -6 to 6
- pulsar_beam: int32 [512], replicated, may hold values from 0 to 1023, as said below
- phase_bin: int32 [512, 32, 4096], P('feed'), may hold values from 0 to 255
Outputs:
- intensity: float32 [1024, 32, 256], P('feed', 'chan')
- folded: float32 [512, 256], P('feed')
The draws below stay inside these ranges and needn't reach their ends.
Inputs may be any that keep to these rules, and one draw needn't show every extreme that they name: For pulsars n in one block of 16 consecutive indices, the number whose pulsar_beam lies in one block of 32 consecutive rows is 0 or exactly 2.
All inputs are finite; a program needn't handle non-finite values.
Results may differ from the reference program's by a relative error of at most 0.007.
Values may be sent and summed in bfloat16 or wider, within the bound.
A program may use at most 128 MiB of HBM per device.

```python
import math
import jax
import jax.numpy as jnp
from jax import lax

F = 1024
NBIN = 256
DS = 16
SEND_CAP = 2
TIME = 4096
PSR_DEV = 16
FEED_DEV = 32
CH = 32
NPSR = 512
N_FEED = 32


def draw_pulsar_beam(key, part):
    key = jax.random.fold_in(key, 11)
    key_favor, key_score, key_shuffle, key_offset = jax.random.split(key, 4)
    holders = F // FEED_DEV
    per_owner = PSR_DEV // SEND_CAP
    favored = jax.random.permutation(key_favor, holders) < 3
    jitter = jax.random.randint(key_score, (holders, holders), 0, 32)
    score = (jitter + jnp.where(favored, 64, 0)[None, :]) * holders + jnp.arange(holders)[None, :]
    ranked = jnp.argsort(-score, axis=1)
    chosen = ranked[:, :per_owner]
    spread = jnp.repeat(chosen, SEND_CAP, axis=1)
    shuffle_keys = jax.random.randint(key_shuffle, (holders, PSR_DEV), 0, 1 << 20) * PSR_DEV + jnp.arange(PSR_DEV)[None, :]
    shuffle = jnp.argsort(shuffle_keys, axis=1)
    placed = jnp.take_along_axis(spread, shuffle, axis=1)
    offset = jax.random.randint(key_offset, (holders, PSR_DEV), 0, FEED_DEV)
    return (placed * FEED_DEV + offset).reshape(-1).astype(jnp.int32)


def set_ends(drawn, stream_key, least, largest):
    shape = drawn.shape
    spot = [jax.random.randint(jax.random.fold_in(stream_key, axis), (), 0, shape[axis]) for axis in range(len(shape))]
    drawn = drawn.at[tuple(spot)].set(least)
    longest = shape.index(max(shape))
    spot[longest] = (spot[longest] + 1) % shape[longest]
    return drawn.at[tuple(spot)].set(largest)


def block_levels(key, dims, cuts, smallest, largest):
    def one(dim, shards_of):
        heights = jax.random.uniform(jax.random.fold_in(jax.random.fold_in(key, 6), dim), (shards_of,), jnp.float32, smallest / len(cuts), largest / len(cuts))
        return jnp.repeat(jnp.exp(heights), dims[dim] // shards_of).reshape((-1,) + (1,) * (len(dims) - dim - 1))

    factor_of = one(*cuts[0])
    for cut in cuts[1:]:
        factor_of = factor_of * one(*cut)
    return factor_of


def normal_values(stream_key, shape, deviation, limit, pieces=(), held_as=jnp.bfloat16):
    values = deviation * jax.random.normal(stream_key, shape, jnp.float32)
    if pieces:
        values = values * block_levels(stream_key, shape, pieces, -0.22, 0.18)
    return jnp.clip(values, -limit, limit).astype(held_as)


def setup_inputs(seed: int = 0) -> dict:
    key_list = jax.random.split(jax.random.key(seed), 4)
    volt = normal_values(key_list[0], (2, F, CH, TIME), 1.0, 6.0, ((1, 32), (2, 4)))
    pulsar_beam = draw_pulsar_beam(jax.random.fold_in(key_list[3], 71), 0)
    phase_bin = set_ends(jax.random.randint(key_list[2], (NPSR, CH, TIME), 0, NBIN), jax.random.fold_in(key_list[2], 1), 0, NBIN - 1).astype(jnp.int32)
    return {"volt": volt, "pulsar_beam": pulsar_beam, "phase_bin": phase_bin}


def reverse_bits(number, bit_count):
    result = jnp.zeros_like(number)
    for shift_bit in range(bit_count):
        result = result + ((number >> shift_bit & 1) << bit_count - 1 - shift_bit)
    return result

def make_weights(beam_group, blocks, per_block, transform_len):
    beam_idx = jnp.arange(per_block, dtype=jnp.int32)[:, None]
    feed_idx = jnp.arange(per_block, dtype=jnp.int32)[None, :]
    phase_step = feed_idx[None] * (beam_group[:, None, None] + blocks * beam_idx[None]) % transform_len
    angle = -2.0 * math.pi * phase_step.astype(jnp.float32) / transform_len
    factor = 1.0 / math.sqrt(transform_len)
    cos_part = (jnp.cos(angle) * factor).astype(jnp.bfloat16)
    sin_part = (jnp.sin(angle) * factor).astype(jnp.bfloat16)
    first = jnp.stack([cos_part, -sin_part], axis=2)
    second = jnp.stack([sin_part, cos_part], axis=2)
    return jnp.stack([first, second], axis=1)

def dif_section(signal, half_span):
    blocks = signal.shape[1]
    sectioned = signal.reshape(2, blocks // (2 * half_span), 2, half_span, -1).astype(jnp.float32)
    lower_re, lower_im = (sectioned[0, :, 0], sectioned[1, :, 0])
    upper_re, upper_im = (sectioned[0, :, 1], sectioned[1, :, 1])
    angle = -math.pi * jnp.arange(half_span, dtype=jnp.float32) / half_span
    turn_re = jnp.cos(angle)[:, None]
    turn_im = jnp.sin(angle)[:, None]
    diff_re = lower_re - upper_re
    diff_im = lower_im - upper_im
    summed = jnp.stack([lower_re + upper_re, lower_im + upper_im])
    differenced = jnp.stack([diff_re * turn_re - diff_im * turn_im, diff_re * turn_im + diff_im * turn_re])
    return jnp.stack([summed, differenced], axis=2).reshape(signal.shape).astype(jnp.bfloat16)

def reference(volt, pulsar_beam, phase_bin):
    blocks = N_FEED
    per_block = FEED_DEV
    bit_count = blocks.bit_length() - 1
    weights = make_weights(reverse_bits(jnp.arange(blocks, dtype=jnp.int32), bit_count), blocks, per_block, F)
    weights_wide = weights.astype(jnp.float32)

    def per_channel(channel):
        signal = lax.dynamic_index_in_dim(volt, channel, 2, keepdims=False)
        sectioned = signal.reshape(2, blocks, -1)
        for level_bit in reversed(range(bit_count)):
            sectioned = dif_section(sectioned, 1 << level_bit)
        sectioned = sectioned.reshape(2, blocks, per_block, TIME).astype(jnp.float32)
        formed = jnp.einsum('pakbl,bplt->apkt', weights_wide, sectioned).astype(jnp.bfloat16).astype(jnp.float32)
        detected = (formed[0] * formed[0] + formed[1] * formed[1]).reshape(F, TIME)
        averaged = detected.reshape(F, TIME // DS, DS).sum(-1) * (1.0 / DS)
        tracks = jnp.take(detected.astype(jnp.bfloat16), pulsar_beam, axis=0)
        return (averaged, tracks)
    averaged, tracks = lax.map(per_channel, jnp.arange(CH, dtype=jnp.int32))
    intensity = jnp.transpose(averaged, (1, 0, 2))
    tracks = jnp.transpose(tracks, (1, 0, 2)).astype(jnp.float32)

    def fold_one(series, indices):
        return jax.ops.segment_sum(series.reshape(-1), indices.reshape(-1), num_segments=NBIN)
    profile = jax.vmap(fold_one)(tracks, phase_bin)
    folded = profile * (NBIN / (CH * TIME))
    return (intensity, folded)
```

```python
import functools
import math

import jax
import jax.numpy as jnp
import ml_dtypes
import numpy as np
from jax import lax
from jax.experimental import pallas as pl
from jax.experimental.pallas import tpu as pltpu
from jax.sharding import PartitionSpec as P

F = 1024
NBIN = 256
DS = 16
BLK = 32
CHD = 8
TD = 128
NP = 8
CUT = 4
PIECE = 16 // CUT
CUT2 = 4
PIECE2 = NP // CUT2
MESH = pl.DeviceIdType.MESH
F32 = jnp.float32
BF16 = jnp.bfloat16


def reverse_bits(number, bit_count):
    return sum((number >> b & 1) << bit_count - 1 - b for b in range(bit_count))


def tables():
    idx = np.arange(BLK)
    rev = np.array([reverse_bits(i, 5) for i in range(BLK)])

    def spread(out_idx):
        angle = 2.0 * math.pi * (np.outer(out_idx, idx) % BLK) / BLK
        cos, sin = np.cos(angle), np.sin(angle)
        parts = np.array([[cos, sin], [-sin, cos]])
        return parts

    eye = np.eye(CHD)
    first = np.einsum("aboi,cd->aocibd", spread(rev), eye).reshape(512, 512)
    second = np.einsum("aboi,cd->aocbid", spread(idx), eye).reshape(512, 512)
    step = np.exp(-2j * math.pi * rev / F)
    step = np.stack([step.real, step.imag])[:, :, None, None] * np.ones((1, 1, CHD, TD))
    avg = np.zeros((8, 2, TD, 8, 2, TD // DS))
    for j in range(8):
        for b in range(2):
            for t in range(TD):
                avg[j, b, t, j, b, t // DS] = 1.0 / DS
    avg = avg.reshape(8, 2 * TD, TD)
    bf = ml_dtypes.bfloat16
    return first.astype(bf), second.astype(bf), step.astype(np.float32), avg.astype(bf)


def routes():
    found = []
    for dz in (0, 1, 3, 2):
        for dx in (0, 1, 3, 2):
            for dc in (0, 1):
                if (dz, dx, dc) != (0, 0, 0):
                    found.append((dz, dx, dc))
    hops = {0: 0, 1: 1, 3: 1, 2: 2}
    found.sort(key=lambda r: -(hops[r[0]] + hops[r[1]]))
    return found


def kernel(
    volt,
    beam,
    phase,
    first_in,
    second_in,
    step_in,
    avg_in,
    inten_out,
    folded_out,
    recv,
    mid,
    det,
    tracks,
    rtracks,
    inten,
    rinten,
    acc,
    bins,
    high,
    low,
    grid,
    rows,
    part,
    parts,
    first,
    second,
    step,
    avg,
    turn,
    local_sem,
    send_sem,
    recv_sem,
    send2_sem,
    recv2_sem,
    send3_sem,
    recv3_sem,
    send4_sem,
    recv4_sem,
):
    me = lax.axis_index("feed")
    chan = lax.axis_index("chan")
    core = me % 2
    x = me // 2 % 4
    z = me // 8

    def towards(route):
        dz, dx, dc = route
        return (((z + dz) % 4) * 4 + (x + dx) % 4) * 2 + (core + dc) % 2

    barrier = pltpu.get_barrier_semaphore()
    for route in routes():
        pl.semaphore_signal(
            barrier, inc=1, device_id=(chan, towards(route)), device_id_type=MESH
        )
    for dy in range(1, 4):
        pl.semaphore_signal(
            barrier, inc=1, device_id=((chan + dy) % 4, me), device_id_type=MESH
        )
    own = pltpu.make_async_copy(
        volt.at[:, :, :, pl.ds(pl.multiple_of(me * TD, TD), TD)], recv.at[me], local_sem.at[0]
    )
    own.start()
    loads = [
        pltpu.make_async_copy(first_in, first, local_sem.at[1]),
        pltpu.make_async_copy(step_in, step, local_sem.at[2]),
        pltpu.make_async_copy(
            phase.at[:, pl.ds(pl.multiple_of(chan * CHD, CHD), CHD), :], bins, local_sem.at[3]
        ),
        pltpu.make_async_copy(second_in, second, local_sem.at[4]),
        pltpu.make_async_copy(avg_in, avg, local_sem.at[5]),
    ]
    pl.semaphore_wait(barrier, 34)

    def send_piece(c, carry):
        for route in routes():
            there = towards(route)
            pltpu.make_async_remote_copy(
                src_ref=volt.at[
                    :, pl.ds(c * PIECE, PIECE), :, pl.ds(pl.multiple_of(there * TD, TD), TD)
                ],
                dst_ref=recv.at[me, :, pl.ds(c * PIECE, PIECE)],
                send_sem=send_sem,
                recv_sem=recv_sem.at[c],
                device_id=(chan, there),
                device_id_type=MESH,
            ).start()
        return carry

    lax.fori_loop(0, CUT, send_piece, 0)
    for load in loads:
        load.start()

    loads[2].wait()

    def digits(n, carry):
        pair = jnp.concatenate([bins[n], bins[n + NP]], axis=0)
        high[n] = (pair >> 4).astype(F32).astype(BF16)
        low[n] = (pair & 15).astype(F32).astype(BF16)
        return carry

    lax.fori_loop(0, NP, digits, 0)
    acc[...] = jnp.zeros_like(acc)
    turn[0] = jnp.full((BLK, CHD, TD), 1.0 / 32.0, F32)
    turn[1] = jnp.zeros((BLK, CHD, TD), F32)
    loads[0].wait()
    loads[1].wait()
    own.wait()

    def section(i, carry):
        both = recv[:, :, i].astype(F32).reshape(2 * BLK, 2, CHD, TD)
        operand = jnp.concatenate(
            [both[:, 0].reshape(512, TD), both[:, 1].reshape(512, TD)], axis=1
        ).astype(BF16)
        result = jnp.dot(first[...], operand, preferred_element_type=F32)
        done = []
        for e in range(2):
            value = result[:, e * TD : (e + 1) * TD].reshape(2, BLK, CHD, TD)
            tr, ti = turn[0], turn[1]
            done.append((value[0] * tr - value[1] * ti, value[0] * ti + value[1] * tr))
            sr, si = step[0], step[1]
            turn[0] = tr * sr - ti * si
            turn[1] = tr * si + ti * sr
        for a in range(2):
            mid[:, a, i] = (
                jnp.concatenate([done[0][a], done[1][a]], axis=1).astype(BF16)
            )
        return carry

    for c in range(CUT):
        span = recv.at[pl.ds(0, BLK - 1), :, pl.ds(c * PIECE, PIECE)]
        pltpu.make_async_copy(span, span, recv_sem.at[c]).wait()
        lax.fori_loop(c * PIECE, (c + 1) * PIECE, section, 0)

    loads[3].wait()
    loads[4].wait()

    def form(j, carry):
        operand = jnp.concatenate(
            [mid[2 * j].reshape(512, TD), mid[2 * j + 1].reshape(512, TD)], axis=1
        )
        result = jnp.dot(second[...], operand, preferred_element_type=F32)
        power = result[:256] * result[:256] + result[256:] * result[256:]
        det[pl.ds(2 * j * BLK, BLK)] = power[:, :TD].reshape(BLK, CHD, TD)
        det[pl.ds((2 * j + 1) * BLK, BLK)] = power[:, TD:].reshape(BLK, CHD, TD)
        acc[j // 8] += jnp.dot(power.astype(BF16), avg[j % 8], preferred_element_type=F32)
        return carry

    lax.fori_loop(0, BLK // 2, form, 0)

    def pick(d, carry):
        for n in range(NP):
            lo_row = det[beam[d * 2 * NP + n]]
            hi_row = det[beam[d * 2 * NP + NP + n]]
            tracks[d, n] = jnp.concatenate([lo_row, hi_row], axis=0).astype(BF16)
        return carry

    lax.fori_loop(0, BLK, pick, 0)
    rtracks[me] = tracks[me]

    def send_tracks(c, carry):
        for route in routes():
            there = towards(route)
            pltpu.make_async_remote_copy(
                src_ref=tracks.at[there, pl.ds(c * PIECE2, PIECE2)],
                dst_ref=rtracks.at[me, pl.ds(c * PIECE2, PIECE2)],
                send_sem=send2_sem,
                recv_sem=recv2_sem.at[c],
                device_id=(chan, there),
                device_id_type=MESH,
            ).start()
        return carry

    lax.fori_loop(0, CUT2, send_tracks, 0)
    for half in range(2):
        inten[pl.ds(16 * half, 16)] = acc[half].T.reshape(16, TD // DS, 256)
    rinten[me] = inten[me]
    for route in routes():
        there = towards(route)
        pltpu.make_async_remote_copy(
            src_ref=inten.at[there],
            dst_ref=rinten.at[me],
            send_sem=send3_sem,
            recv_sem=recv3_sem,
            device_id=(chan, there),
            device_id_type=MESH,
        ).start()

    same = (
        lax.broadcasted_iota(jnp.int32, (256, 256), 0) % 16
        == lax.broadcasted_iota(jnp.int32, (256, 256), 1) % 16
    )
    zero = jnp.zeros((16, TD), BF16)
    one = jnp.ones((16, TD), BF16)

    def fold(n, carry):
        grid[...] = jnp.zeros_like(grid)

        def fold_part(s, carry):
            left, right = [], []
            for e in range(8):
                series = rtracks[s * 8 + e, n]
                span = pl.ds(pl.multiple_of((s * 8 + e) * TD, TD), TD)
                low_now = low[n, :, span]
                high_now = high[n, :, span]
                left.append(
                    jnp.concatenate(
                        [jnp.where(low_now == v, series, zero) for v in range(16)], axis=0
                    )
                )
                right.append(
                    jnp.concatenate(
                        [jnp.where(high_now == v, one, zero) for v in range(16)], axis=0
                    )
                )
            grid[...] += lax.dot_general(
                jnp.concatenate(left, axis=1),
                jnp.concatenate(right, axis=1),
                (((1,), (1,)), ((), ())),
                preferred_element_type=F32,
            )
            return carry

        lax.fori_loop(0, 4, fold_part, 0)
        kept = jnp.where(same, grid[...], 0.0).reshape(BLK, CHD, 256)
        rows[:, pl.ds(n, 1), :] = jnp.sum(kept, axis=1, keepdims=True)
        return carry

    for c in range(CUT2):
        span = rtracks.at[pl.ds(0, BLK - 1), pl.ds(c * PIECE2, PIECE2)]
        pltpu.make_async_copy(span, span, recv2_sem.at[c]).wait()
        lax.fori_loop(c * PIECE2, (c + 1) * PIECE2, fold, 0)

    lane = lax.broadcasted_iota(jnp.int32, (1, 1, 256), 2)
    level = rows[...]
    for d in (8, 4, 2, 1):
        count = 2 * d
        upper = (lane // d) % 2 == 1
        lower_part, upper_part = level[:count], level[count:]
        stay = jnp.where(upper, upper_part, lower_part)
        move = jnp.where(upper, lower_part, upper_part)
        flat = move.reshape(count * NP, 256)
        down = pltpu.roll(flat, d, 1).reshape(count, NP, 256)
        up = pltpu.roll(flat, 256 - d, 1).reshape(count, NP, 256)
        level = stay + jnp.where(upper, down, up)
    part[...] = level.reshape(2 * NP, 256) * (NBIN / (4 * CHD * 4096.0))
    for dy in range(1, 4):
        pltpu.make_async_remote_copy(
            src_ref=part,
            dst_ref=parts.at[dy - 1],
            send_sem=send4_sem,
            recv_sem=recv4_sem.at[dy - 1],
            device_id=((chan + dy) % 4, me),
            device_id_type=MESH,
        ).start()

    span = rinten.at[pl.ds(0, BLK - 1)]
    pltpu.make_async_copy(span, span, recv3_sem).wait()
    inten_out[...] = rinten[...].reshape(256, 256).T.reshape(BLK, CHD, 256)
    for dy in range(1, 4):
        pltpu.make_async_copy(part, parts.at[dy - 1], recv4_sem.at[dy - 1]).wait()
    folded_out[...] = part[...] + parts[0] + parts[1] + parts[2]

    span = recv.at[pl.ds(0, BLK - 1)]
    pltpu.make_async_copy(span, span, send_sem).wait()
    span = rtracks.at[pl.ds(0, BLK - 1)]
    pltpu.make_async_copy(span, span, send2_sem).wait()
    span = rinten.at[pl.ds(0, BLK - 1)]
    pltpu.make_async_copy(span, span, send3_sem).wait()
    pltpu.make_async_copy(parts, parts, send4_sem).wait()


def shards(volt, pulsar_beam, phase_bin):
    first, second, step, avg = tables()
    anywhere = pl.BlockSpec(memory_space=pl.ANY)
    whole = pl.BlockSpec(memory_space=pltpu.VMEM)
    dma = pltpu.SemaphoreType.DMA
    return pl.pallas_call(
        kernel,
        out_shape=(
            jax.ShapeDtypeStruct((BLK, CHD, 4096 // DS), F32),
            jax.ShapeDtypeStruct((2 * NP, NBIN), F32),
        ),
        in_specs=[anywhere, pl.BlockSpec(memory_space=pltpu.SMEM)] + [anywhere] * 5,
        out_specs=(whole, whole),
        scratch_shapes=[
            pltpu.VMEM((BLK, 2, 16, 16, TD), BF16),
            pltpu.VMEM((BLK, 2, 16, 16, TD), BF16),
            pltpu.VMEM((F, CHD, TD), F32),
            pltpu.VMEM((BLK, NP, 16, TD), BF16),
            pltpu.VMEM((BLK, NP, 16, TD), BF16),
            pltpu.VMEM((BLK, TD // DS, 256), F32),
            pltpu.VMEM((BLK, TD // DS, 256), F32),
            pltpu.VMEM((2, 256, TD), F32),
            pltpu.VMEM((2 * NP, CHD, 4096), jnp.int32),
            pltpu.VMEM((NP, 16, 4096), BF16),
            pltpu.VMEM((NP, 16, 4096), BF16),
            pltpu.VMEM((256, 256), F32),
            pltpu.VMEM((BLK, NP, 256), F32),
            pltpu.VMEM((2 * NP, 256), F32),
            pltpu.VMEM((3, 2 * NP, 256), F32),
            pltpu.VMEM((512, 512), BF16),
            pltpu.VMEM((512, 512), BF16),
            pltpu.VMEM((2, BLK, CHD, TD), F32),
            pltpu.VMEM((8, 2 * TD, TD), BF16),
            pltpu.VMEM((2, BLK, CHD, TD), F32),
            dma((6,)),
            dma(()),
            dma((CUT,)),
            dma(()),
            dma((CUT2,)),
            dma(()),
            dma(()),
            dma(()),
            dma((3,)),
        ],
        compiler_params=pltpu.CompilerParams(
            collective_id=0, has_side_effects=True, vmem_limit_bytes=50 * 1024 * 1024
        ),
        name="beams",
    )(
        volt.reshape(2, 16, 16, 4096),
        pulsar_beam,
        phase_bin,
        jnp.asarray(first),
        jnp.asarray(second),
        jnp.asarray(step),
        jnp.asarray(avg),
    )


def solution(mesh):
    placed = (P(None, "feed", "chan", None), P(), P("feed", None, None))
    return jax.shard_map(
        shards,
        mesh=mesh,
        in_specs=placed,
        out_specs=(P("feed", "chan", None), P("feed", None)),
        check_vma=False,
    )
```

```python
import math

import jax
import jax.numpy as jnp
import ml_dtypes
import numpy as np
from jax import lax
from jax.experimental import pallas as pl
from jax.experimental.pallas import tpu as pltpu
from jax.sharding import PartitionSpec as P

F = 1024
NBIN = 256
DS = 16
TIME = 4096
BLK = 32
CHD = 8
TD = 128
PSR = 16
NQ = 4
PAIRS = 16
CUT = 4
PIECE = PAIRS // CUT
CUT2 = 2
PIECE2 = NQ // CUT2
SUMS = TD // DS
MESH = pl.DeviceIdType.MESH
F32 = jnp.float32
BF16 = jnp.bfloat16


def reverse_bits(number, bit_count):
    return sum((number >> b & 1) << bit_count - 1 - b for b in range(bit_count))


def tables():
    idx = np.arange(BLK)
    rev = np.array([reverse_bits(i, 5) for i in range(BLK)])

    def transform(out_idx):
        angle = 2.0 * math.pi * (np.outer(out_idx, idx) % BLK) / BLK
        cos, sin = np.cos(angle), np.sin(angle)
        return np.array([[cos, sin], [-sin, cos]])

    first = np.einsum("aboi,cd->aocibd", transform(rev), np.eye(8)).reshape(512, 512)
    within = transform(idx).reshape(2, 2, BLK, PAIRS, 2)
    second = np.einsum("aboij,cd->aocibjd", within, np.eye(4)).reshape(256, 256)
    step = np.exp(-2j * math.pi * 2 * rev / F)[:, None] * np.ones((1, 8))
    start = np.exp(-2j * math.pi * np.outer(rev, np.arange(8) // 4) / F) / 32.0
    turns = np.stack([step.real, step.imag, start.real, start.imag])
    turns = turns[..., None] * np.ones(TD)
    avg = np.zeros((4, 4, TD, 16, SUMS))
    for j in range(4):
        for b in range(4):
            for t in range(TD):
                avg[j, b, t, 4 * j + b, t // DS] = 1.0 / DS
    avg = avg.reshape(4, 4 * TD, TD)
    bf = ml_dtypes.bfloat16
    return first.astype(bf), second.astype(bf), turns.astype(np.float32), avg.astype(bf)


def routes():
    hops = {0: 0, 1: 1, 3: 1, 2: 2}
    found = [
        (dz, dx, dc)
        for dz in (0, 1, 3, 2)
        for dx in (0, 1, 3, 2)
        for dc in (0, 1)
        if (dz, dx, dc) != (0, 0, 0)
    ]
    found.sort(key=lambda r: -(hops[r[0]] + hops[r[1]]))
    return found


def halves(low_rows, high_rows):
    upper = lax.broadcasted_iota(jnp.int32, low_rows.shape, low_rows.ndim - 2) >= 4
    axis = low_rows.ndim - 2
    return (
        jnp.where(upper, pltpu.roll(high_rows, 4, axis), low_rows),
        jnp.where(upper, high_rows, pltpu.roll(low_rows, 4, axis)),
    )


def kernel(
    volt,
    beam_in,
    phase,
    first_in,
    second_in,
    turns_in,
    avg_in,
    inten_out,
    folded_out,
    held,
    sent,
    recv,
    mid,
    det,
    tracks,
    rtracks,
    inten,
    rinten,
    acc,
    bins,
    high,
    low,
    grid,
    part,
    parts,
    first,
    second,
    turns,
    avg,
    turn,
    beam,
    local_sem,
    held_sem,
    send_sem,
    recv_sem,
    send2_sem,
    recv2_sem,
    send3_sem,
    recv3_sem,
    send4_sem,
    recv4_sem,
):
    me = lax.axis_index("feed")
    chan = lax.axis_index("chan")
    core = me % 2
    x = me // 2 % 4
    z = me // 8

    def towards(route):
        dz, dx, dc = route
        return (((z + dz) % 4) * 4 + (x + dx) % 4) * 2 + (core + dc) % 2

    barrier = pltpu.get_barrier_semaphore()
    for route in routes():
        pl.semaphore_signal(
            barrier, inc=1, device_id=(chan, towards(route)), device_id_type=MESH
        )
    for dy in range(1, 4):
        pl.semaphore_signal(
            barrier, inc=1, device_id=((chan + dy) % 4, me), device_id_type=MESH
        )
    reads = []
    for c in range(CUT):
        span = pl.ds(c * PIECE, PIECE)
        reads.append(pltpu.make_async_copy(volt.at[:, span], held.at[:, span], held_sem.at[c]))
        reads[-1].start()
    loads = [
        pltpu.make_async_copy(first_in, first, local_sem.at[0]),
        pltpu.make_async_copy(turns_in, turns, local_sem.at[1]),
        pltpu.make_async_copy(
            phase.at[:, pl.ds(pl.multiple_of(chan * CHD, CHD), CHD), :], bins, local_sem.at[2]
        ),
        pltpu.make_async_copy(second_in, second, local_sem.at[3]),
        pltpu.make_async_copy(avg_in, avg, local_sem.at[4]),
        pltpu.make_async_copy(beam_in, beam, local_sem.at[5]),
    ]
    for load in loads:
        load.start()

    def arrange(i, carry):
        real = held[0, i].astype(F32)
        imag = held[1, i].astype(F32)
        real0, real1 = halves(real[:8], real[8:])
        imag0, imag1 = halves(imag[:8], imag[8:])
        for h, tile in enumerate(((real0, imag0), (real1, imag1))):
            tile = jnp.concatenate(tile, axis=0).astype(BF16)
            for d in range(BLK):
                sent[h, d, i] = tile[:, d * TD : (d + 1) * TD]
        return carry

    def send(h, c):
        for route in routes():
            there = towards(route)
            pltpu.make_async_remote_copy(
                src_ref=sent.at[h, there, pl.ds(c * PIECE, PIECE)],
                dst_ref=recv.at[h, me, pl.ds(c * PIECE, PIECE)],
                send_sem=send_sem,
                recv_sem=recv_sem.at[h * CUT + c],
                device_id=(chan, there),
                device_id_type=MESH,
            ).start()

    for c in range(CUT):
        reads[c].wait()
        lax.fori_loop(c * PIECE, (c + 1) * PIECE, arrange, 0)
        if c == 0:
            pl.semaphore_wait(barrier, 34)
        send(0, c)
    own = pltpu.make_async_copy(sent.at[:, me], recv.at[:, me], local_sem.at[6])
    own.start()

    def send_later(c, carry):
        send(1, c)
        return carry

    lax.fori_loop(0, CUT, send_later, 0)

    loads[2].wait()

    def digits(q, carry):
        top0, top1 = halves(bins[q], bins[q + 4])
        bottom0, bottom1 = halves(bins[q + 8], bins[q + 12])
        for h, tile in enumerate(((top0, bottom0), (top1, bottom1))):
            tile = jnp.concatenate(tile, axis=0)
            high[h, q] = (tile >> 4).astype(F32).astype(BF16)
            low[h, q] = (tile & 15).astype(F32).astype(BF16)
        return carry

    lax.fori_loop(0, NQ, digits, 0)
    acc[...] = jnp.zeros_like(acc)
    grid[...] = jnp.zeros_like(grid)
    for load in loads[:2] + loads[3:]:
        load.wait()
    own.wait()

    def sections(h):
        turn[...] = turns[2:]

        def section(i, carry):
            operand = jnp.concatenate(
                [recv[h, :, 2 * i + e].reshape(512, TD) for e in range(2)], axis=1
            )
            result = jnp.dot(first[...], operand, preferred_element_type=F32)
            for e in range(2):
                value = result[:, e * TD : (e + 1) * TD].reshape(2, BLK, 8, TD)
                tr, ti = turn[0], turn[1]
                turned = (value[0] * tr - value[1] * ti, value[0] * ti + value[1] * tr)
                mid[:, 2 * i + e] = jnp.concatenate(turned, axis=1).astype(BF16)
                sr, si = turns[0], turns[1]
                turn[0] = tr * sr - ti * si
                turn[1] = tr * si + ti * sr
            return carry

        for c in range(CUT):
            span = recv.at[h, pl.ds(0, BLK - 1), pl.ds(c * PIECE, PIECE)]
            pltpu.make_async_copy(span, span, recv_sem.at[h * CUT + c]).wait()
            lax.fori_loop(c * PIECE // 2, (c + 1) * PIECE // 2, section, 0)

    def forms(h):
        def form(j, carry):
            operand = jnp.concatenate(
                [mid[4 * j + b].reshape(256, TD) for b in range(4)], axis=1
            )
            result = jnp.dot(second[...], operand, preferred_element_type=F32)
            power = result[:128] * result[:128] + result[128:] * result[128:]
            for b in range(4):
                place = pl.multiple_of(8 + (4 * j + b) * 128, 8)
                det[pl.ds(place, 128), :] = power[:, b * TD : (b + 1) * TD]
            acc[h, j // 4] += jnp.dot(power.astype(BF16), avg[j % 4], preferred_element_type=F32)
            return carry

        lax.fori_loop(0, BLK // 4, form, 0)

    upper_rows = lax.broadcasted_iota(jnp.int32, (8, TD), 0) >= 4

    def picks(h):
        def pick(d, carry):
            for q in range(NQ):
                found = []
                for n in range(4):
                    row = beam[d * PSR + 4 * n + q]
                    found.append(det[pl.ds(8 + 4 * row - 4 * (n % 2), 8), :])
                tile = [jnp.where(upper_rows, found[n + 1], found[n]) for n in (0, 2)]
                tracks[h, d, q] = jnp.concatenate(tile, axis=0).astype(BF16)
            return carry

        lax.fori_loop(0, BLK, pick, 0)
        rtracks[h, me] = tracks[h, me]

        def send_tracks(c, carry):
            for route in routes():
                there = towards(route)
                pltpu.make_async_remote_copy(
                    src_ref=tracks.at[h, there, pl.ds(c * PIECE2, PIECE2)],
                    dst_ref=rtracks.at[h, me, pl.ds(c * PIECE2, PIECE2)],
                    send_sem=send2_sem,
                    recv_sem=recv2_sem.at[h * CUT2 + c],
                    device_id=(chan, there),
                    device_id_type=MESH,
                ).start()
            return carry

        lax.fori_loop(0, CUT2, send_tracks, 0)

    zero = jnp.zeros((16, TD), BF16)
    one = jnp.ones((16, TD), BF16)

    def folds(h, c):
        def fold(step, carry):
            q = step // 4
            s = step % 4
            left, right = [], []
            for e in range(8):
                series = rtracks[h, s * 8 + e, q]
                span = pl.ds(pl.multiple_of((s * 8 + e) * TD, TD), TD)
                low_now = low[h, q, :, span]
                high_now = high[h, q, :, span]
                left.append(
                    jnp.concatenate(
                        [jnp.where(low_now == v, series, zero) for v in range(16)], axis=0
                    )
                )
                right.append(
                    jnp.concatenate(
                        [jnp.where(high_now == v, one, zero) for v in range(16)], axis=0
                    )
                )
            grid[q] += lax.dot_general(
                jnp.concatenate(left, axis=1),
                jnp.concatenate(right, axis=1),
                (((1,), (1,)), ((), ())),
                preferred_element_type=F32,
            )
            return carry

        span = rtracks.at[h, pl.ds(0, BLK - 1), pl.ds(c * PIECE2, PIECE2)]
        pltpu.make_async_copy(span, span, recv2_sem.at[h * CUT2 + c]).wait()
        lax.fori_loop(c * PIECE2 * 4, (c + 1) * PIECE2 * 4, fold, 0)

    sections(0)
    forms(0)
    picks(0)
    sections(1)
    forms(1)
    picks(1)

    for g in range(2):
        both = [acc[h, g].T.reshape(16, SUMS, TD) for h in range(2)]
        inten[pl.ds(16 * g, 16)] = jnp.concatenate(both, axis=1).astype(BF16)
    rinten[me] = inten[me]
    for route in routes():
        there = towards(route)
        pltpu.make_async_remote_copy(
            src_ref=inten.at[there],
            dst_ref=rinten.at[me],
            send_sem=send3_sem,
            recv_sem=recv3_sem,
            device_id=(chan, there),
            device_id_type=MESH,
        ).start()

    for h in range(2):
        for c in range(CUT2):
            folds(h, c)

    same = (
        lax.broadcasted_iota(jnp.int32, (256, 256), 0) % 16
        == lax.broadcasted_iota(jnp.int32, (256, 256), 1) % 16
    )
    lane = lax.broadcasted_iota(jnp.int32, (1, 1, 256), 2)
    sub = lax.broadcasted_iota(jnp.int32, (2, 8, 256), 1)
    total = jnp.zeros((2, 8, 256), F32)
    for q in range(NQ):
        level = jnp.where(same, grid[q], 0.0).reshape(32, 8, 256)
        for d in (8, 4, 2, 1):
            count = 2 * d
            upper = (lane // d) % 2 == 1
            lower_part, upper_part = level[:count], level[count:]
            stay = jnp.where(upper, upper_part, lower_part)
            flat = jnp.where(upper, lower_part, upper_part).reshape(count * 8, 256)
            down = pltpu.roll(flat, d, 1).reshape(count, 8, 256)
            up = pltpu.roll(flat, 256 - d, 1).reshape(count, 8, 256)
            level = stay + jnp.where(upper, down, up)
        level = level + pltpu.roll(level, 6, 1)
        level = level + pltpu.roll(level, 7, 1)
        level = jnp.where(sub % 4 == 0, level, 0.0)
        total = total + (pltpu.roll(level, q, 1) if q else level)
    part[...] = total.reshape(PSR, NBIN) * (NBIN / (4 * CHD * float(TIME)))
    for dy in range(1, 4):
        pltpu.make_async_remote_copy(
            src_ref=part,
            dst_ref=parts.at[dy - 1],
            send_sem=send4_sem,
            recv_sem=recv4_sem.at[dy - 1],
            device_id=((chan + dy) % 4, me),
            device_id_type=MESH,
        ).start()

    span = rinten.at[pl.ds(0, BLK - 1)]
    pltpu.make_async_copy(span, span, recv3_sem).wait()
    averages = rinten[...].astype(F32)
    sides = [
        averages[:, h * SUMS : (h + 1) * SUMS].reshape(256, TD).T.reshape(16, 8, 256)
        for h in range(2)
    ]
    even, odd = halves(*sides)
    inten_out[...] = jnp.stack([even, odd], axis=1).reshape(BLK, CHD, 256)
    for dy in range(1, 4):
        pltpu.make_async_copy(part, parts.at[dy - 1], recv4_sem.at[dy - 1]).wait()
    folded_out[...] = part[...] + parts[0] + parts[1] + parts[2]

    span = recv.at[:, pl.ds(0, BLK - 1)]
    pltpu.make_async_copy(span, span, send_sem).wait()
    span = rtracks.at[:, pl.ds(0, BLK - 1)]
    pltpu.make_async_copy(span, span, send2_sem).wait()
    span = rinten.at[pl.ds(0, BLK - 1)]
    pltpu.make_async_copy(span, span, send3_sem).wait()
    pltpu.make_async_copy(parts, parts, send4_sem).wait()


def shards(volt, pulsar_beam, phase_bin):
    first, second, turns, avg = tables()
    far = pl.BlockSpec(memory_space=pltpu.HBM)
    whole = pl.BlockSpec(memory_space=pltpu.VMEM)
    dma = pltpu.SemaphoreType.DMA
    return pl.pallas_call(
        kernel,
        out_shape=(
            jax.ShapeDtypeStruct((BLK, CHD, TIME // DS), F32),
            jax.ShapeDtypeStruct((PSR, NBIN), F32),
        ),
        in_specs=[far] * 7,
        out_specs=(whole, whole),
        scratch_shapes=[
            pltpu.VMEM((2, PAIRS, 16, TIME), BF16),
            pltpu.VMEM((2, BLK, PAIRS, 16, TD), BF16),
            pltpu.VMEM((2, BLK, PAIRS, 16, TD), BF16),
            pltpu.VMEM((BLK, PAIRS, 16, TD), BF16),
            pltpu.VMEM((8 + 4 * F + 8, TD), F32),
            pltpu.VMEM((2, BLK, NQ, 16, TD), BF16),
            pltpu.VMEM((2, BLK, NQ, 16, TD), BF16),
            pltpu.VMEM((BLK, 2 * SUMS, TD), BF16),
            pltpu.VMEM((BLK, 2 * SUMS, TD), BF16),
            pltpu.VMEM((2, 2, TD, TD), F32),
            pltpu.VMEM((PSR, CHD, TIME), jnp.int32),
            pltpu.VMEM((2, NQ, 16, TIME), BF16),
            pltpu.VMEM((2, NQ, 16, TIME), BF16),
            pltpu.VMEM((NQ, 256, 256), F32),
            pltpu.VMEM((PSR, NBIN), F32),
            pltpu.VMEM((3, PSR, NBIN), F32),
            pltpu.VMEM((512, 512), BF16),
            pltpu.VMEM((256, 256), BF16),
            pltpu.VMEM((4, BLK, 8, TD), F32),
            pltpu.VMEM((4, 4 * TD, TD), BF16),
            pltpu.VMEM((2, BLK, 8, TD), F32),
            pltpu.SMEM((512,), jnp.int32),
            dma((7,)),
            dma((CUT,)),
            dma(()),
            dma((2 * CUT,)),
            dma(()),
            dma((2 * CUT2,)),
            dma(()),
            dma(()),
            dma(()),
            dma((3,)),
        ],
        compiler_params=pltpu.CompilerParams(
            collective_id=0, has_side_effects=True, vmem_limit_bytes=64 * 1024 * 1024
        ),
        name="beams",
    )(
        volt.reshape(2, PAIRS, 16, TIME),
        pulsar_beam,
        phase_bin,
        jnp.asarray(first),
        jnp.asarray(second),
        jnp.asarray(turns),
        jnp.asarray(avg),
    )


def solution(mesh):
    placed = (P(None, "feed", "chan", None), P(), P("feed", None, None))
    return jax.shard_map(
        shards,
        mesh=mesh,
        in_specs=placed,
        out_specs=(P("feed", "chan", None), P("feed", None)),
        check_vma=False,
    )
```

```python
import math

import jax
import jax.numpy as jnp
import ml_dtypes
import numpy as np
from jax import lax
from jax.experimental import pallas as pl
from jax.experimental.pallas import tpu as pltpu
from jax.sharding import PartitionSpec as P

F = 1024
NBIN = 256
DS = 16
TIME = 4096
BLK = 32
CHD = 8
TD = 128
PSR = 16
NQ = 4
PAIRS = 16
PIECES = (((0, 2), (2, 2), (4, 4), (8, 4), (12, 4)), ((0, 4), (4, 4), (8, 4), (12, 2), (14, 2)))
CUT = 5
HOLD = 4
WIDE = 16
STEPS = BLK // WIDE
CHUNKS = (((0, 4),), ((0, 2), (2, 2)))
SUMS = TD // DS
MESH = pl.DeviceIdType.MESH
F32 = jnp.float32
BF16 = jnp.bfloat16


def reverse_bits(number, bit_count):
    return sum((number >> b & 1) << bit_count - 1 - b for b in range(bit_count))


def tables():
    idx = np.arange(BLK)
    rev = np.array([reverse_bits(i, 5) for i in range(BLK)])

    def transform(out_idx):
        angle = 2.0 * math.pi * (np.outer(out_idx, idx) % BLK) / BLK
        cos, sin = np.cos(angle), np.sin(angle)
        return np.array([[cos, sin], [-sin, cos]])

    first = np.einsum("aboi,cd->aocibd", transform(rev), np.eye(8)).reshape(512, 512)
    within = transform(idx).reshape(2, 2, BLK, PAIRS, 2)
    second = np.einsum("aboij,cd->aocibjd", within, np.eye(4)).reshape(256, 256)
    step = np.exp(-2j * math.pi * 2 * rev / F)[:, None] * np.ones((1, 8))
    start = np.exp(-2j * math.pi * np.outer(rev, np.arange(8) // 4) / F) / 32.0
    turns = np.stack([step.real, step.imag, start.real, start.imag])
    turns = turns[..., None] * np.ones(TD)
    avg = np.zeros((4, 4, TD, 16, SUMS))
    for j in range(4):
        for b in range(4):
            for t in range(TD):
                avg[j, b, t, 4 * j + b, t // DS] = 1.0 / DS
    avg = avg.reshape(4, 4 * TD, TD)
    bf = ml_dtypes.bfloat16
    return first.astype(bf), second.astype(bf), turns.astype(np.float32), avg.astype(bf)


def routes():
    hops = {0: 0, 1: 1, 3: 1, 2: 2}
    found = [
        (dz, dx, dc)
        for dz in (0, 1, 3, 2)
        for dx in (0, 1, 3, 2)
        for dc in (0, 1)
        if (dz, dx, dc) != (0, 0, 0)
    ]
    found.sort(key=lambda r: -(hops[r[0]] + hops[r[1]]))
    return found


def halves(low_rows, high_rows):
    upper = lax.broadcasted_iota(jnp.int32, low_rows.shape, low_rows.ndim - 2) >= 4
    axis = low_rows.ndim - 2
    return (
        jnp.where(upper, pltpu.roll(high_rows, 4, axis), low_rows),
        jnp.where(upper, high_rows, pltpu.roll(low_rows, 4, axis)),
    )


def kernel(
    volt,
    beam_in,
    phase,
    first_in,
    second_in,
    turns_in,
    avg_in,
    inten_out,
    folded_out,
    held,
    sent,
    recv,
    mid,
    det,
    tracks,
    rtracks,
    inten,
    rinten,
    acc,
    bins,
    low,
    right,
    grid,
    part,
    parts,
    first,
    second,
    turns,
    avg,
    turn,
    beam,
    local_sem,
    held_sem,
    send_sem,
    recv_sem,
    send2_sem,
    recv2_sem,
    send3_sem,
    recv3_sem,
    send4_sem,
    recv4_sem,
):
    me = lax.axis_index("feed")
    chan = lax.axis_index("chan")
    core = me % 2
    x = me // 2 % 4
    z = me // 8

    def towards(route):
        dz, dx, dc = route
        return (((z + dz) % 4) * 4 + (x + dx) % 4) * 2 + (core + dc) % 2

    barrier = pltpu.get_barrier_semaphore()
    for route in routes():
        pl.semaphore_signal(
            barrier, inc=1, device_id=(chan, towards(route)), device_id_type=MESH
        )
    for dy in range(1, 4):
        pl.semaphore_signal(
            barrier, inc=1, device_id=((chan + dy) % 4, me), device_id_type=MESH
        )
    reads = []
    for c, piece in enumerate(PIECES[0]):
        span = pl.ds(*piece)
        reads.append(pltpu.make_async_copy(volt.at[:, span], held.at[:, span], held_sem.at[c]))
        reads[-1].start()
    loads = [
        pltpu.make_async_copy(first_in, first, local_sem.at[0]),
        pltpu.make_async_copy(turns_in, turns, local_sem.at[1]),
        pltpu.make_async_copy(
            phase.at[:, pl.ds(pl.multiple_of(chan * CHD, CHD), CHD), :], bins, local_sem.at[2]
        ),
        pltpu.make_async_copy(second_in, second, local_sem.at[3]),
        pltpu.make_async_copy(avg_in, avg, local_sem.at[4]),
        pltpu.make_async_copy(beam_in, beam, local_sem.at[5]),
    ]
    for load in loads:
        load.start()

    def arrange(i, carry):
        real = held[0, i].astype(F32)
        imag = held[1, i].astype(F32)
        real0, real1 = halves(real[:8], real[8:])
        imag0, imag1 = halves(imag[:8], imag[8:])
        for h, tile in enumerate(((real0, imag0), (real1, imag1))):
            tile = jnp.concatenate(tile, axis=0).astype(BF16)
            for d in range(BLK):
                sent[h, d, i] = tile[:, d * TD : (d + 1) * TD]
        return carry

    def send(h, c, first_pair, count):
        for route in routes():
            there = towards(route)
            pltpu.make_async_remote_copy(
                src_ref=sent.at[h, there, pl.ds(first_pair, count)],
                dst_ref=recv.at[h, me, pl.ds(first_pair, count)],
                send_sem=send_sem,
                recv_sem=recv_sem.at[h * CUT + c],
                device_id=(chan, there),
                device_id_type=MESH,
            ).start()

    for c, (first_pair, count) in enumerate(PIECES[0]):
        reads[c].wait()
        lax.fori_loop(first_pair, first_pair + count, arrange, 0)
        if c == 0:
            pl.semaphore_wait(barrier, 34)
        send(0, c, first_pair, count)
    own = pltpu.make_async_copy(sent.at[:, me], recv.at[:, me], local_sem.at[6])
    own.start()

    def send_later(c, carry):
        send(1, c, c * 4, 4)
        return carry

    lax.fori_loop(0, 3, send_later, 0)
    send(1, 3, 12, 2)
    send(1, 4, 14, 2)

    zero = jnp.zeros((16, TD), BF16)
    one = jnp.ones((16, TD), BF16)
    loads[2].wait()

    def digits(step, carry):
        q = step // 4
        span = pl.ds(pl.multiple_of(step % 4 * 8 * TD, 8 * TD), 8 * TD)
        top0, top1 = halves(bins[q, :, span], bins[q + 4, :, span])
        bottom0, bottom1 = halves(bins[q + 8, :, span], bins[q + 12, :, span])
        for h, tile in enumerate(((top0, bottom0), (top1, bottom1))):
            tile = jnp.concatenate(tile, axis=0)
            low[h, q, :, span] = (tile & 15).astype(F32).astype(BF16)
            high = (tile >> 4).astype(F32).astype(BF16)
            marks = [
                jnp.concatenate(
                    [
                        jnp.where(high[:, e * TD : (e + 1) * TD] == v, one, zero)
                        for v in range(16)
                    ],
                    axis=0,
                )
                for e in range(8)
            ]
            right[h, q, span, :] = jnp.concatenate(marks, axis=1).T
        return carry

    lax.fori_loop(0, 4 * NQ, digits, 0)
    acc[...] = jnp.zeros_like(acc)
    grid[...] = jnp.zeros_like(grid)
    for load in loads[:2] + loads[3:]:
        load.wait()
    own.wait()

    def sections(h, before=None, then=None):
        turn[...] = turns[2:]

        def section(i, carry):
            operand = jnp.concatenate(
                [recv[h, :, 2 * i + e].reshape(512, TD) for e in range(2)], axis=1
            )
            result = jnp.dot(first[...], operand, preferred_element_type=F32)
            for e in range(2):
                value = result[:, e * TD : (e + 1) * TD].reshape(2, BLK, 8, TD)
                tr, ti = turn[0], turn[1]
                turned = (value[0] * tr - value[1] * ti, value[0] * ti + value[1] * tr)
                mid[:, 2 * i + e] = jnp.concatenate(turned, axis=1).astype(BF16)
                sr, si = turns[0], turns[1]
                turn[0] = tr * sr - ti * si
                turn[1] = tr * si + ti * sr
            return carry

        for c, (first_pair, count) in enumerate(PIECES[h]):
            if c == before:
                then()
            span = recv.at[h, pl.ds(0, BLK - 1), pl.ds(first_pair, count)]
            pltpu.make_async_copy(span, span, recv_sem.at[h * CUT + c]).wait()
            lax.fori_loop(first_pair // 2, (first_pair + count) // 2, section, 0)

    def forms(h):
        def form(j, carry):
            operand = jnp.concatenate(
                [mid[4 * j + b].reshape(256, TD) for b in range(4)], axis=1
            )
            result = jnp.dot(second[...], operand, preferred_element_type=F32)
            power = result[:128] * result[:128] + result[128:] * result[128:]
            for b in range(4):
                place = pl.multiple_of(8 + (4 * j + b) * 128, 8)
                det[pl.ds(place, 128), :] = power[:, b * TD : (b + 1) * TD]
            acc[h, j // 4] += jnp.dot(power.astype(BF16), avg[j % 4], preferred_element_type=F32)
            return carry

        lax.fori_loop(0, BLK // 4, form, 0)

    upper_rows = lax.broadcasted_iota(jnp.int32, (8, TD), 0) >= 4

    def picks(h):
        def pick(d, carry):
            for q in range(NQ):
                found = []
                for n in range(4):
                    row = beam[d * PSR + 4 * n + q]
                    found.append(det[pl.ds(8 + 4 * row - 4 * (n % 2), 8), :])
                tile = [jnp.where(upper_rows, found[n + 1], found[n]) for n in (0, 2)]
                tracks[h, d, q] = jnp.concatenate(tile, axis=0).astype(BF16)
            return carry

        lax.fori_loop(0, BLK, pick, 0)
        rtracks[h, me] = tracks[h, me]

    def send_tracks(h):
        for c, (first_group, count) in enumerate(CHUNKS[h]):
            for route in routes():
                there = towards(route)
                pltpu.make_async_remote_copy(
                    src_ref=tracks.at[h, there, pl.ds(first_group, count)],
                    dst_ref=rtracks.at[h, me, pl.ds(first_group, count)],
                    send_sem=send2_sem,
                    recv_sem=recv2_sem.at[h + c],
                    device_id=(chan, there),
                    device_id_type=MESH,
                ).start()

    def folds(h, c, first_group, count):
        def fold(step, carry):
            q = step // STEPS
            s = step % STEPS
            left = []
            for e in range(WIDE):
                series = rtracks[h, s * WIDE + e, q]
                low_now = low[h, q, :, pl.ds(pl.multiple_of((s * WIDE + e) * TD, TD), TD)]
                left.append(
                    jnp.concatenate(
                        [jnp.where(low_now == v, series, zero) for v in range(16)], axis=0
                    )
                )
            span = pl.ds(pl.multiple_of(s * WIDE * TD, WIDE * TD), WIDE * TD)
            grid[q] += jnp.dot(
                jnp.concatenate(left, axis=1), right[h, q, span, :], preferred_element_type=F32
            )
            return carry

        span = rtracks.at[h, pl.ds(0, BLK - 1), pl.ds(first_group, count)]
        pltpu.make_async_copy(span, span, recv2_sem.at[h + c]).wait()
        lax.fori_loop(first_group * STEPS, (first_group + count) * STEPS, fold, 0)

    sections(0)
    forms(0)
    picks(0)
    sections(1, HOLD, lambda: send_tracks(0))
    forms(1)
    picks(1)
    send_tracks(1)

    for g in range(2):
        both = [acc[h, g].T.reshape(16, SUMS, TD) for h in range(2)]
        inten[pl.ds(16 * g, 16)] = jnp.concatenate(both, axis=1).astype(BF16)
    rinten[me] = inten[me]
    for route in routes():
        there = towards(route)
        pltpu.make_async_remote_copy(
            src_ref=inten.at[there],
            dst_ref=rinten.at[me],
            send_sem=send3_sem,
            recv_sem=recv3_sem,
            device_id=(chan, there),
            device_id_type=MESH,
        ).start()

    same = (
        lax.broadcasted_iota(jnp.int32, (256, 256), 0) % 16
        == lax.broadcasted_iota(jnp.int32, (256, 256), 1) % 16
    )
    lane = lax.broadcasted_iota(jnp.int32, (1, 1, 256), 2)
    sub = lax.broadcasted_iota(jnp.int32, (2, 8, 256), 1)

    def profile(q):
        level = jnp.where(same, grid[q], 0.0).reshape(32, 8, 256)
        for d in (8, 4, 2, 1):
            count = 2 * d
            upper = (lane // d) % 2 == 1
            lower_part, upper_part = level[:count], level[count:]
            stay = jnp.where(upper, upper_part, lower_part)
            flat = jnp.where(upper, lower_part, upper_part).reshape(count * 8, 256)
            down = pltpu.roll(flat, d, 1).reshape(count, 8, 256)
            up = pltpu.roll(flat, 256 - d, 1).reshape(count, 8, 256)
            level = stay + jnp.where(upper, down, up)
        level = level + pltpu.roll(level, 6, 1)
        level = level + pltpu.roll(level, 7, 1)
        level = jnp.where(sub % 4 == 0, level, 0.0)
        return pltpu.roll(level, q, 1) if q else level

    folds(0, 0, 0, 4)
    total = jnp.zeros((2, 8, 256), F32)
    for c, (first_group, count) in enumerate(CHUNKS[1]):
        folds(1, c, first_group, count)
        for q in range(first_group, first_group + count):
            total = total + profile(q)
    part[...] = total.reshape(PSR, NBIN) * (NBIN / (4 * CHD * float(TIME)))
    for dy in range(1, 4):
        pltpu.make_async_remote_copy(
            src_ref=part,
            dst_ref=parts.at[dy - 1],
            send_sem=send4_sem,
            recv_sem=recv4_sem.at[dy - 1],
            device_id=((chan + dy) % 4, me),
            device_id_type=MESH,
        ).start()

    span = rinten.at[pl.ds(0, BLK - 1)]
    pltpu.make_async_copy(span, span, recv3_sem).wait()
    averages = rinten[...].astype(F32)
    sides = [
        averages[:, h * SUMS : (h + 1) * SUMS].reshape(256, TD).T.reshape(16, 8, 256)
        for h in range(2)
    ]
    even, odd = halves(*sides)
    inten_out[...] = jnp.stack([even, odd], axis=1).reshape(BLK, CHD, 256)
    for dy in range(1, 4):
        pltpu.make_async_copy(part, parts.at[dy - 1], recv4_sem.at[dy - 1]).wait()
    folded_out[...] = part[...] + parts[0] + parts[1] + parts[2]

    span = recv.at[:, pl.ds(0, BLK - 1)]
    pltpu.make_async_copy(span, span, send_sem).wait()
    span = rtracks.at[:, pl.ds(0, BLK - 1)]
    pltpu.make_async_copy(span, span, send2_sem).wait()
    span = rinten.at[pl.ds(0, BLK - 1)]
    pltpu.make_async_copy(span, span, send3_sem).wait()
    pltpu.make_async_copy(parts, parts, send4_sem).wait()


def shards(volt, pulsar_beam, phase_bin):
    first, second, turns, avg = tables()
    far = pl.BlockSpec(memory_space=pltpu.HBM)
    whole = pl.BlockSpec(memory_space=pltpu.VMEM)
    dma = pltpu.SemaphoreType.DMA
    return pl.pallas_call(
        kernel,
        out_shape=(
            jax.ShapeDtypeStruct((BLK, CHD, TIME // DS), F32),
            jax.ShapeDtypeStruct((PSR, NBIN), F32),
        ),
        in_specs=[far] * 7,
        out_specs=(whole, whole),
        scratch_shapes=[
            pltpu.VMEM((2, PAIRS, 16, TIME), BF16),
            pltpu.VMEM((2, BLK, PAIRS, 16, TD), BF16),
            pltpu.VMEM((2, BLK, PAIRS, 16, TD), BF16),
            pltpu.VMEM((BLK, PAIRS, 16, TD), BF16),
            pltpu.VMEM((8 + 4 * F + 8, TD), F32),
            pltpu.VMEM((2, BLK, NQ, 16, TD), BF16),
            pltpu.VMEM((2, BLK, NQ, 16, TD), BF16),
            pltpu.VMEM((BLK, 2 * SUMS, TD), BF16),
            pltpu.VMEM((BLK, 2 * SUMS, TD), BF16),
            pltpu.VMEM((2, 2, TD, TD), F32),
            pltpu.VMEM((PSR, CHD, TIME), jnp.int32),
            pltpu.VMEM((2, NQ, 16, TIME), BF16),
            pltpu.VMEM((2, NQ, TIME, 256), BF16),
            pltpu.VMEM((NQ, 256, 256), F32),
            pltpu.VMEM((PSR, NBIN), F32),
            pltpu.VMEM((3, PSR, NBIN), F32),
            pltpu.VMEM((512, 512), BF16),
            pltpu.VMEM((256, 256), BF16),
            pltpu.VMEM((4, BLK, 8, TD), F32),
            pltpu.VMEM((4, 4 * TD, TD), BF16),
            pltpu.VMEM((2, BLK, 8, TD), F32),
            pltpu.SMEM((512,), jnp.int32),
            dma((7,)),
            dma((CUT,)),
            dma(()),
            dma((2 * CUT,)),
            dma(()),
            dma((3,)),
            dma(()),
            dma(()),
            dma(()),
            dma((3,)),
        ],
        compiler_params=pltpu.CompilerParams(
            collective_id=0, has_side_effects=True, vmem_limit_bytes=50 * 1024 * 1024
        ),
        name="beams",
    )(
        *(
            pltpu.with_memory_space_constraint(operand, pltpu.HBM)
            for operand in (
                volt.reshape(2, PAIRS, 16, TIME),
                pulsar_beam,
                phase_bin,
                jnp.asarray(first),
                jnp.asarray(second),
                jnp.asarray(turns),
                jnp.asarray(avg),
            )
        )
    )


def solution(mesh):
    placed = (P(None, "feed", "chan", None), P(), P("feed", None, None))
    return jax.shard_map(
        shards,
        mesh=mesh,
        in_specs=placed,
        out_specs=(P("feed", "chan", None), P("feed", None)),
        check_vma=False,
    )
```

```python
import math

import jax
import jax.numpy as jnp
import ml_dtypes
import numpy as np
from jax import lax
from jax.experimental import pallas as pl
from jax.experimental.pallas import tpu as pltpu
from jax.sharding import PartitionSpec as P

F = 1024
NBIN = 256
DS = 16
TIME = 4096
BLK = 32
CHD = 8
TD = 128
PSR = 16
NQ = 4
PAIRS = 16
PIECES = (((0, 2), (2, 2), (4, 4), (8, 4), (12, 4)), ((0, 4), (4, 4), (8, 4), (12, 2), (14, 2)))
CUT = 5
HOLD = 4
WIDE = 16
STEPS = BLK // WIDE
CHUNKS = (((0, 4),), ((0, 2), (2, 1), (3, 1)))
SUMS = TD // DS
MESH = pl.DeviceIdType.MESH
F32 = jnp.float32
BF16 = jnp.bfloat16


def reverse_bits(number, bit_count):
    return sum((number >> b & 1) << bit_count - 1 - b for b in range(bit_count))


def tables():
    idx = np.arange(BLK)
    rev = np.array([reverse_bits(i, 5) for i in range(BLK)])

    def transform(out_idx):
        angle = 2.0 * math.pi * (np.outer(out_idx, idx) % BLK) / BLK
        cos, sin = np.cos(angle), np.sin(angle)
        return np.array([[cos, sin], [-sin, cos]])

    first = np.einsum("aboi,cd->aocibd", transform(rev), np.eye(8)).reshape(512, 512)
    within = transform(idx).reshape(2, 2, BLK, PAIRS, 2)
    second = np.einsum("aboij,cd->aocibjd", within, np.eye(4)).reshape(256, 256)
    step = np.exp(-2j * math.pi * 2 * rev / F)[:, None] * np.ones((1, 8))
    start = np.exp(-2j * math.pi * np.outer(rev, np.arange(8) // 4) / F) / 32.0
    turns = np.stack([step.real, step.imag, start.real, start.imag])
    turns = turns[..., None] * np.ones(TD)
    avg = np.zeros((4, 4, TD, 16, SUMS))
    for j in range(4):
        for b in range(4):
            for t in range(TD):
                avg[j, b, t, 4 * j + b, t // DS] = 1.0 / DS
    avg = avg.reshape(4, 4 * TD, TD)
    bf = ml_dtypes.bfloat16
    return first.astype(bf), second.astype(bf), turns.astype(np.float32), avg.astype(bf)


def routes():
    hops = {0: 0, 1: 1, 3: 1, 2: 2}
    found = [
        (dz, dx, dc)
        for dz in (0, 1, 3, 2)
        for dx in (0, 1, 3, 2)
        for dc in (0, 1)
        if (dz, dx, dc) != (0, 0, 0)
    ]
    found.sort(key=lambda r: -(hops[r[0]] + hops[r[1]]))
    return found


def halves(low_rows, high_rows):
    upper = lax.broadcasted_iota(jnp.int32, low_rows.shape, low_rows.ndim - 2) >= 4
    axis = low_rows.ndim - 2
    return (
        jnp.where(upper, pltpu.roll(high_rows, 4, axis), low_rows),
        jnp.where(upper, high_rows, pltpu.roll(low_rows, 4, axis)),
    )


def kernel(
    volt,
    beam_in,
    phase,
    first_in,
    second_in,
    turns_in,
    avg_in,
    inten_out,
    folded_out,
    held,
    sent,
    recv,
    mid,
    det,
    tracks,
    rtracks,
    inten,
    rinten,
    acc,
    bins,
    low,
    right,
    grid,
    part,
    parts,
    first,
    second,
    turns,
    avg,
    turn,
    beam,
    local_sem,
    held_sem,
    send_sem,
    recv_sem,
    send2_sem,
    recv2_sem,
    send3_sem,
    recv3_sem,
    send4_sem,
    recv4_sem,
):
    me = lax.axis_index("feed")
    chan = lax.axis_index("chan")
    core = me % 2
    x = me // 2 % 4
    z = me // 8

    def towards(route):
        dz, dx, dc = route
        return (((z + dz) % 4) * 4 + (x + dx) % 4) * 2 + (core + dc) % 2

    barrier = pltpu.get_barrier_semaphore()
    for route in routes():
        pl.semaphore_signal(
            barrier, inc=1, device_id=(chan, towards(route)), device_id_type=MESH
        )
    for dy in range(1, 4):
        pl.semaphore_signal(
            barrier, inc=1, device_id=((chan + dy) % 4, me), device_id_type=MESH
        )
    reads = []
    for c, piece in enumerate(PIECES[0]):
        span = pl.ds(*piece)
        reads.append(pltpu.make_async_copy(volt.at[:, span], held.at[:, span], held_sem.at[c]))
        reads[-1].start()
    loads = [
        pltpu.make_async_copy(first_in, first, local_sem.at[0]),
        pltpu.make_async_copy(turns_in, turns, local_sem.at[1]),
        pltpu.make_async_copy(
            phase.at[:, pl.ds(pl.multiple_of(chan * CHD, CHD), CHD), :], bins, local_sem.at[2]
        ),
        pltpu.make_async_copy(second_in, second, local_sem.at[3]),
        pltpu.make_async_copy(avg_in, avg, local_sem.at[4]),
        pltpu.make_async_copy(beam_in, beam, local_sem.at[5]),
    ]
    for load in loads:
        load.start()

    def arrange(i, carry):
        real = held[0, i].astype(F32)
        imag = held[1, i].astype(F32)
        real0, real1 = halves(real[:8], real[8:])
        imag0, imag1 = halves(imag[:8], imag[8:])
        for h, tile in enumerate(((real0, imag0), (real1, imag1))):
            tile = jnp.concatenate(tile, axis=0).astype(BF16)
            for d in range(BLK):
                sent[h, d, i] = tile[:, d * TD : (d + 1) * TD]
        return carry

    def send(h, c, first_pair, count):
        for route in routes():
            there = towards(route)
            pltpu.make_async_remote_copy(
                src_ref=sent.at[h, there, pl.ds(first_pair, count)],
                dst_ref=recv.at[h, me, pl.ds(first_pair, count)],
                send_sem=send_sem,
                recv_sem=recv_sem.at[h * CUT + c],
                device_id=(chan, there),
                device_id_type=MESH,
            ).start()

    for c, (first_pair, count) in enumerate(PIECES[0]):
        reads[c].wait()
        lax.fori_loop(first_pair, first_pair + count, arrange, 0)
        if c == 0:
            pl.semaphore_wait(barrier, 34)
        send(0, c, first_pair, count)
    own = pltpu.make_async_copy(sent.at[:, me], recv.at[:, me], local_sem.at[6])
    own.start()

    def send_later(c, carry):
        send(1, c, c * 4, 4)
        return carry

    lax.fori_loop(0, 3, send_later, 0)
    send(1, 3, 12, 2)
    send(1, 4, 14, 2)

    zero = jnp.zeros((16, TD), BF16)
    one = jnp.ones((16, TD), BF16)
    loads[2].wait()

    def digits(step, carry):
        q = step // 4
        span = pl.ds(pl.multiple_of(step % 4 * 8 * TD, 8 * TD), 8 * TD)
        top0, top1 = halves(bins[q, :, span], bins[q + 4, :, span])
        bottom0, bottom1 = halves(bins[q + 8, :, span], bins[q + 12, :, span])
        for h, tile in enumerate(((top0, bottom0), (top1, bottom1))):
            tile = jnp.concatenate(tile, axis=0)
            low[h, q, :, span] = (tile & 15).astype(F32).astype(BF16)
            high = (tile >> 4).astype(F32).astype(BF16)
            marks = [
                jnp.concatenate(
                    [
                        jnp.where(high[:, e * TD : (e + 1) * TD] == v, one, zero)
                        for v in range(16)
                    ],
                    axis=0,
                )
                for e in range(8)
            ]
            right[h, q, span, :] = jnp.concatenate(marks, axis=1).T
        return carry

    lax.fori_loop(0, 4 * NQ, digits, 0)
    acc[...] = jnp.zeros_like(acc)
    grid[...] = jnp.zeros_like(grid)
    for load in loads[:2] + loads[3:]:
        load.wait()
    own.wait()

    def sections(h, before=None, then=None):
        turn[...] = turns[2:]

        def section(i, carry):
            operand = jnp.concatenate(
                [recv[h, :, 2 * i + e].reshape(512, TD) for e in range(2)], axis=1
            )
            result = jnp.dot(first[...], operand, preferred_element_type=F32)
            for e in range(2):
                value = result[:, e * TD : (e + 1) * TD].reshape(2, BLK, 8, TD)
                tr, ti = turn[0], turn[1]
                turned = (value[0] * tr - value[1] * ti, value[0] * ti + value[1] * tr)
                mid[:, 2 * i + e] = jnp.concatenate(turned, axis=1).astype(BF16)
                sr, si = turns[0], turns[1]
                turn[0] = tr * sr - ti * si
                turn[1] = tr * si + ti * sr
            return carry

        for c, (first_pair, count) in enumerate(PIECES[h]):
            if c == before:
                then()
            span = recv.at[h, pl.ds(0, BLK - 1), pl.ds(first_pair, count)]
            pltpu.make_async_copy(span, span, recv_sem.at[h * CUT + c]).wait()
            lax.fori_loop(first_pair // 2, (first_pair + count) // 2, section, 0)

    def forms(h):
        def form(j, carry):
            operand = jnp.concatenate(
                [mid[4 * j + b].reshape(256, TD) for b in range(4)], axis=1
            )
            result = jnp.dot(second[...], operand, preferred_element_type=F32)
            power = result[:128] * result[:128] + result[128:] * result[128:]
            for b in range(4):
                place = pl.multiple_of(8 + (4 * j + b) * 128, 8)
                det[pl.ds(place, 128), :] = power[:, b * TD : (b + 1) * TD]
            acc[h, j // 4] += jnp.dot(power.astype(BF16), avg[j % 4], preferred_element_type=F32)
            return carry

        lax.fori_loop(0, BLK // 4, form, 0, unroll=2)

    upper_rows = lax.broadcasted_iota(jnp.int32, (8, TD), 0) >= 4

    def picks(h):
        def pick(d, carry):
            for q in range(NQ):
                found = []
                for n in range(4):
                    row = beam[d * PSR + 4 * n + q]
                    found.append(det[pl.ds(8 + 4 * row - 4 * (n % 2), 8), :])
                tile = [jnp.where(upper_rows, found[n + 1], found[n]) for n in (0, 2)]
                tracks[h, d, q] = jnp.concatenate(tile, axis=0).astype(BF16)
            return carry

        lax.fori_loop(0, BLK, pick, 0)
        rtracks[h, me] = tracks[h, me]

    def send_tracks(h):
        for c, (first_group, count) in enumerate(CHUNKS[h]):
            for route in routes():
                there = towards(route)
                pltpu.make_async_remote_copy(
                    src_ref=tracks.at[h, there, pl.ds(first_group, count)],
                    dst_ref=rtracks.at[h, me, pl.ds(first_group, count)],
                    send_sem=send2_sem,
                    recv_sem=recv2_sem.at[h + c],
                    device_id=(chan, there),
                    device_id_type=MESH,
                ).start()

    def folds(h, c, first_group, count):
        def fold(step, carry):
            q = step // STEPS
            s = step % STEPS
            left = []
            for e in range(WIDE):
                series = rtracks[h, s * WIDE + e, q]
                low_now = low[h, q, :, pl.ds(pl.multiple_of((s * WIDE + e) * TD, TD), TD)]
                left.append(
                    jnp.concatenate(
                        [jnp.where(low_now == v, series, zero) for v in range(16)], axis=0
                    )
                )
            span = pl.ds(pl.multiple_of(s * WIDE * TD, WIDE * TD), WIDE * TD)
            grid[q] += jnp.dot(
                jnp.concatenate(left, axis=1), right[h, q, span, :], preferred_element_type=F32
            )
            return carry

        span = rtracks.at[h, pl.ds(0, BLK - 1), pl.ds(first_group, count)]
        pltpu.make_async_copy(span, span, recv2_sem.at[h + c]).wait()
        lax.fori_loop(first_group * STEPS, (first_group + count) * STEPS, fold, 0)

    sections(0)
    forms(0)
    picks(0)
    sections(1, HOLD, lambda: send_tracks(0))
    forms(1)
    picks(1)
    send_tracks(1)

    for g in range(2):
        both = [acc[h, g].T.reshape(16, SUMS, TD) for h in range(2)]
        inten[pl.ds(16 * g, 16)] = jnp.concatenate(both, axis=1).astype(BF16)
    rinten[me] = inten[me]
    for route in routes():
        there = towards(route)
        pltpu.make_async_remote_copy(
            src_ref=inten.at[there],
            dst_ref=rinten.at[me],
            send_sem=send3_sem,
            recv_sem=recv3_sem,
            device_id=(chan, there),
            device_id_type=MESH,
        ).start()

    same = (
        lax.broadcasted_iota(jnp.int32, (256, 256), 0) % 16
        == lax.broadcasted_iota(jnp.int32, (256, 256), 1) % 16
    )
    lane = lax.broadcasted_iota(jnp.int32, (1, 1, 1, 256), 3)
    sub = lax.broadcasted_iota(jnp.int32, (2, 8, 256), 1)

    def profile(first_group, count):
        level = grid[pl.ds(first_group, count)]
        level = jnp.where(same, level, 0.0).reshape(count, 32, 8, 256)
        for d in (8, 4, 2, 1):
            upper = (lane // d) % 2 == 1
            lower_part, upper_part = level[:, : 2 * d], level[:, 2 * d :]
            stay = jnp.where(upper, upper_part, lower_part)
            flat = jnp.where(upper, lower_part, upper_part).reshape(count * 2 * d * 8, 256)
            down = pltpu.roll(flat, d, 1).reshape(count, 2 * d, 8, 256)
            up = pltpu.roll(flat, 256 - d, 1).reshape(count, 2 * d, 8, 256)
            level = stay + jnp.where(upper, down, up)
        found = jnp.zeros((2, 8, 256), F32)
        for q in range(count):
            sums = level[q] + pltpu.roll(level[q], 6, 1)
            sums = sums + pltpu.roll(sums, 7, 1)
            sums = jnp.where(sub % 4 == 0, sums, 0.0)
            found = found + (pltpu.roll(sums, first_group + q, 1) if first_group + q else sums)
        return found

    folds(0, 0, 0, 4)
    total = jnp.zeros((2, 8, 256), F32)
    for c, (first_group, count) in enumerate(CHUNKS[1]):
        folds(1, c, first_group, count)
        total = total + profile(first_group, count)
    part[...] = total.reshape(PSR, NBIN) * (NBIN / (4 * CHD * float(TIME)))
    for dy in range(1, 4):
        pltpu.make_async_remote_copy(
            src_ref=part,
            dst_ref=parts.at[dy - 1],
            send_sem=send4_sem,
            recv_sem=recv4_sem.at[dy - 1],
            device_id=((chan + dy) % 4, me),
            device_id_type=MESH,
        ).start()

    span = rinten.at[pl.ds(0, BLK - 1)]
    pltpu.make_async_copy(span, span, recv3_sem).wait()
    averages = rinten[...].astype(F32)
    sides = [
        averages[:, h * SUMS : (h + 1) * SUMS].reshape(256, TD).T.reshape(16, 8, 256)
        for h in range(2)
    ]
    even, odd = halves(*sides)
    inten_out[...] = jnp.stack([even, odd], axis=1).reshape(BLK, CHD, 256)
    for dy in range(1, 4):
        pltpu.make_async_copy(part, parts.at[dy - 1], recv4_sem.at[dy - 1]).wait()
    folded_out[...] = part[...] + parts[0] + parts[1] + parts[2]

    span = recv.at[:, pl.ds(0, BLK - 1)]
    pltpu.make_async_copy(span, span, send_sem).wait()
    span = rtracks.at[:, pl.ds(0, BLK - 1)]
    pltpu.make_async_copy(span, span, send2_sem).wait()
    span = rinten.at[pl.ds(0, BLK - 1)]
    pltpu.make_async_copy(span, span, send3_sem).wait()
    pltpu.make_async_copy(parts, parts, send4_sem).wait()


def shards(volt, pulsar_beam, phase_bin):
    first, second, turns, avg = tables()
    far = pl.BlockSpec(memory_space=pltpu.HBM)
    whole = pl.BlockSpec(memory_space=pltpu.VMEM)
    dma = pltpu.SemaphoreType.DMA
    return pl.pallas_call(
        kernel,
        out_shape=(
            jax.ShapeDtypeStruct((BLK, CHD, TIME // DS), F32),
            jax.ShapeDtypeStruct((PSR, NBIN), F32),
        ),
        in_specs=[far] * 7,
        out_specs=(whole, whole),
        scratch_shapes=[
            pltpu.VMEM((2, PAIRS, 16, TIME), BF16),
            pltpu.VMEM((2, BLK, PAIRS, 16, TD), BF16),
            pltpu.VMEM((2, BLK, PAIRS, 16, TD), BF16),
            pltpu.VMEM((BLK, PAIRS, 16, TD), BF16),
            pltpu.VMEM((8 + 4 * F + 8, TD), F32),
            pltpu.VMEM((2, BLK, NQ, 16, TD), BF16),
            pltpu.VMEM((2, BLK, NQ, 16, TD), BF16),
            pltpu.VMEM((BLK, 2 * SUMS, TD), BF16),
            pltpu.VMEM((BLK, 2 * SUMS, TD), BF16),
            pltpu.VMEM((2, 2, TD, TD), F32),
            pltpu.VMEM((PSR, CHD, TIME), jnp.int32),
            pltpu.VMEM((2, NQ, 16, TIME), BF16),
            pltpu.VMEM((2, NQ, TIME, 256), BF16),
            pltpu.VMEM((NQ, 256, 256), F32),
            pltpu.VMEM((PSR, NBIN), F32),
            pltpu.VMEM((3, PSR, NBIN), F32),
            pltpu.VMEM((512, 512), BF16),
            pltpu.VMEM((256, 256), BF16),
            pltpu.VMEM((4, BLK, 8, TD), F32),
            pltpu.VMEM((4, 4 * TD, TD), BF16),
            pltpu.VMEM((2, BLK, 8, TD), F32),
            pltpu.SMEM((512,), jnp.int32),
            dma((7,)),
            dma((CUT,)),
            dma(()),
            dma((2 * CUT,)),
            dma(()),
            dma((4,)),
            dma(()),
            dma(()),
            dma(()),
            dma((3,)),
        ],
        compiler_params=pltpu.CompilerParams(
            collective_id=0, has_side_effects=True, vmem_limit_bytes=50 * 1024 * 1024
        ),
        name="beams",
    )(
        *(
            pltpu.with_memory_space_constraint(operand, pltpu.HBM)
            for operand in (
                volt.reshape(2, PAIRS, 16, TIME),
                pulsar_beam,
                phase_bin,
                jnp.asarray(first),
                jnp.asarray(second),
                jnp.asarray(turns),
                jnp.asarray(avg),
            )
        )
    )


def solution(mesh):
    placed = (P(None, "feed", "chan", None), P(), P("feed", None, None))
    return jax.shard_map(
        shards,
        mesh=mesh,
        in_specs=placed,
        out_specs=(P("feed", "chan", None), P("feed", None)),
        check_vma=False,
    )
```

```python
import math

import jax
import jax.numpy as jnp
import ml_dtypes
import numpy as np
from jax import lax
from jax.experimental import pallas as pl
from jax.experimental.pallas import tpu as pltpu
from jax.sharding import PartitionSpec as P

F = 1024
NBIN = 256
DS = 16
TIME = 4096
BLK = 32
CHD = 8
TD = 128
PSR = 16
NQ = 4
PAIRS = 16
PIECES = (((0, 2), (2, 2), (4, 4), (8, 4), (12, 4)), ((0, 4), (4, 4), (8, 4), (12, 2), (14, 2)))
CUT = 5
HOLD = 4
WIDE = 16
STEPS = BLK // WIDE
CHUNKS = (((0, 4),), ((0, 2), (2, 1), (3, 1)))
SUMS = TD // DS
MESH = pl.DeviceIdType.MESH
F32 = jnp.float32
BF16 = jnp.bfloat16


def reverse_bits(number, bit_count):
    return sum((number >> b & 1) << bit_count - 1 - b for b in range(bit_count))


def tables():
    idx = np.arange(BLK)
    rev = np.array([reverse_bits(i, 5) for i in range(BLK)])

    def transform(out_idx):
        angle = 2.0 * math.pi * (np.outer(out_idx, idx) % BLK) / BLK
        cos, sin = np.cos(angle), np.sin(angle)
        return np.array([[cos, sin], [-sin, cos]])

    first = np.einsum("aboi,cd->aocibd", transform(rev), np.eye(8)).reshape(512, 512)
    within = transform(idx).reshape(2, 2, BLK, PAIRS, 2)
    second = np.einsum("aboij,cd->aocibjd", within, np.eye(4)).reshape(256, 256)
    step = np.exp(-2j * math.pi * 2 * rev / F)[:, None] * np.ones((1, 8))
    start = np.exp(-2j * math.pi * np.outer(rev, np.arange(8) // 4) / F) / 32.0
    turns = np.stack([step.real, step.imag, start.real, start.imag])
    turns = turns[..., None] * np.ones(TD)
    avg = np.zeros((4, 4, TD, 16, SUMS))
    for j in range(4):
        for b in range(4):
            for t in range(TD):
                avg[j, b, t, 4 * j + b, t // DS] = 1.0 / DS
    avg = avg.reshape(4, 4 * TD, TD)
    bf = ml_dtypes.bfloat16
    return first.astype(bf), second.astype(bf), turns.astype(np.float32), avg.astype(bf)


def routes():
    rings = (
        ((2, 2),),
        ((1, 2), (2, 1), (3, 2), (2, 3)),
        ((1, 1), (3, 1), (3, 3), (1, 3)),
        ((2, 0), (0, 2)),
        ((1, 0), (0, 1), (3, 0), (0, 3)),
        ((0, 0),),
    )
    found = [(dz, dx, dc) for ring in rings for dc in (0, 1) for dz, dx in ring]
    return [route for route in found if route != (0, 0, 0)]


def halves(low_rows, high_rows):
    upper = lax.broadcasted_iota(jnp.int32, low_rows.shape, low_rows.ndim - 2) >= 4
    axis = low_rows.ndim - 2
    return (
        jnp.where(upper, pltpu.roll(high_rows, 4, axis), low_rows),
        jnp.where(upper, high_rows, pltpu.roll(low_rows, 4, axis)),
    )


def kernel(
    volt,
    beam_in,
    phase,
    first_in,
    second_in,
    turns_in,
    avg_in,
    inten_out,
    folded_out,
    held,
    sent,
    recv,
    mid,
    det,
    tracks,
    rtracks,
    inten,
    rinten,
    acc,
    bins,
    low,
    right,
    grid,
    part,
    parts,
    first,
    second,
    turns,
    avg,
    turn,
    beam,
    local_sem,
    held_sem,
    send_sem,
    recv_sem,
    send2_sem,
    recv2_sem,
    send3_sem,
    recv3_sem,
    send4_sem,
    recv4_sem,
):
    me = lax.axis_index("feed")
    chan = lax.axis_index("chan")
    core = me % 2
    x = me // 2 % 4
    z = me // 8

    def towards(route):
        dz, dx, dc = route
        return (((z + dz) % 4) * 4 + (x + dx) % 4) * 2 + (core + dc) % 2

    reads = []
    for c, piece in enumerate(PIECES[0]):
        span = pl.ds(*piece)
        reads.append(pltpu.make_async_copy(volt.at[:, span], held.at[:, span], held_sem.at[c]))
        reads[-1].start()
    barrier = pltpu.get_barrier_semaphore()
    for route in routes():
        pl.semaphore_signal(
            barrier, inc=1, device_id=(chan, towards(route)), device_id_type=MESH
        )
    for dy in range(1, 4):
        pl.semaphore_signal(
            barrier, inc=1, device_id=((chan + dy) % 4, me), device_id_type=MESH
        )
    loads = [
        pltpu.make_async_copy(first_in, first, local_sem.at[0]),
        pltpu.make_async_copy(turns_in, turns, local_sem.at[1]),
        pltpu.make_async_copy(
            phase.at[:, pl.ds(pl.multiple_of(chan * CHD, CHD), CHD), :], bins, local_sem.at[2]
        ),
        pltpu.make_async_copy(second_in, second, local_sem.at[3]),
        pltpu.make_async_copy(avg_in, avg, local_sem.at[4]),
        pltpu.make_async_copy(beam_in, beam, local_sem.at[5]),
    ]
    for load in loads:
        load.start()

    def arrange(i, carry):
        real = held[0, i].astype(F32)
        imag = held[1, i].astype(F32)
        real0, real1 = halves(real[:8], real[8:])
        imag0, imag1 = halves(imag[:8], imag[8:])
        for h, tile in enumerate(((real0, imag0), (real1, imag1))):
            tile = jnp.concatenate(tile, axis=0).astype(BF16)
            for d in range(BLK):
                sent[h, d, i] = tile[:, d * TD : (d + 1) * TD]
        return carry

    def send(h, c, first_pair, count):
        for route in routes():
            there = towards(route)
            pltpu.make_async_remote_copy(
                src_ref=sent.at[h, there, pl.ds(first_pair, count)],
                dst_ref=recv.at[h, me, pl.ds(first_pair, count)],
                send_sem=send_sem,
                recv_sem=recv_sem.at[h * CUT + c],
                device_id=(chan, there),
                device_id_type=MESH,
            ).start()

    for c, (first_pair, count) in enumerate(PIECES[0]):
        reads[c].wait()
        lax.fori_loop(first_pair, first_pair + count, arrange, 0)
        if c == 0:
            pl.semaphore_wait(barrier, 34)
        send(0, c, first_pair, count)
    own = pltpu.make_async_copy(sent.at[:, me], recv.at[:, me], local_sem.at[6])
    own.start()

    def send_later(c, carry):
        send(1, c, c * 4, 4)
        return carry

    lax.fori_loop(0, 3, send_later, 0)
    send(1, 3, 12, 2)
    send(1, 4, 14, 2)

    zero = jnp.zeros((16, TD), BF16)
    one = jnp.ones((16, TD), BF16)
    loads[2].wait()

    def digits(step, carry):
        q = step // 4
        span = pl.ds(pl.multiple_of(step % 4 * 8 * TD, 8 * TD), 8 * TD)
        top0, top1 = halves(bins[q, :, span], bins[q + 4, :, span])
        bottom0, bottom1 = halves(bins[q + 8, :, span], bins[q + 12, :, span])
        for h, tile in enumerate(((top0, bottom0), (top1, bottom1))):
            tile = jnp.concatenate(tile, axis=0)
            low[h, q, :, span] = (tile & 15).astype(F32).astype(BF16)
            high = (tile >> 4).astype(F32).astype(BF16)
            marks = [
                jnp.concatenate(
                    [
                        jnp.where(high[:, e * TD : (e + 1) * TD] == v, one, zero)
                        for v in range(16)
                    ],
                    axis=0,
                )
                for e in range(8)
            ]
            right[h, q, span, :] = jnp.concatenate(marks, axis=1).T
        return carry

    lax.fori_loop(0, 4 * NQ, digits, 0)
    acc[...] = jnp.zeros_like(acc)
    grid[...] = jnp.zeros_like(grid)
    for load in loads[:2] + loads[3:]:
        load.wait()
    own.wait()

    def sections(h, before=None, then=None):
        turn[...] = turns[2:]

        def section(i, carry):
            operand = jnp.concatenate(
                [recv[h, :, 2 * i + e].reshape(512, TD) for e in range(2)], axis=1
            )
            result = jnp.dot(first[...], operand, preferred_element_type=F32)
            for e in range(2):
                value = result[:, e * TD : (e + 1) * TD].reshape(2, BLK, 8, TD)
                tr, ti = turn[0], turn[1]
                turned = (value[0] * tr - value[1] * ti, value[0] * ti + value[1] * tr)
                mid[:, 2 * i + e] = jnp.concatenate(turned, axis=1).astype(BF16)
                sr, si = turns[0], turns[1]
                turn[0] = tr * sr - ti * si
                turn[1] = tr * si + ti * sr
            return carry

        for c, (first_pair, count) in enumerate(PIECES[h]):
            if c == before:
                then()
            span = recv.at[h, pl.ds(0, BLK - 1), pl.ds(first_pair, count)]
            pltpu.make_async_copy(span, span, recv_sem.at[h * CUT + c]).wait()
            lax.fori_loop(first_pair // 2, (first_pair + count) // 2, section, 0)

    def forms(h):
        def form(j, carry):
            operand = jnp.concatenate(
                [mid[4 * j + b].reshape(256, TD) for b in range(4)], axis=1
            )
            result = jnp.dot(second[...], operand, preferred_element_type=F32)
            power = result[:128] * result[:128] + result[128:] * result[128:]
            for b in range(4):
                place = pl.multiple_of(8 + (4 * j + b) * 128, 8)
                det[pl.ds(place, 128), :] = power[:, b * TD : (b + 1) * TD]
            acc[h, j // 4] += jnp.dot(power.astype(BF16), avg[j % 4], preferred_element_type=F32)
            return carry

        lax.fori_loop(0, BLK // 4, form, 0, unroll=2)

    upper_rows = lax.broadcasted_iota(jnp.int32, (8, TD), 0) >= 4

    def picks(h):
        def pick(d, carry):
            for q in range(NQ):
                found = []
                for n in range(4):
                    row = beam[d * PSR + 4 * n + q]
                    found.append(det[pl.ds(8 + 4 * row - 4 * (n % 2), 8), :])
                tile = [jnp.where(upper_rows, found[n + 1], found[n]) for n in (0, 2)]
                tracks[h, d, q] = jnp.concatenate(tile, axis=0).astype(BF16)
            return carry

        lax.fori_loop(0, BLK, pick, 0)
        rtracks[h, me] = tracks[h, me]

    def send_tracks(h):
        for c, (first_group, count) in enumerate(CHUNKS[h]):
            for route in routes():
                there = towards(route)
                pltpu.make_async_remote_copy(
                    src_ref=tracks.at[h, there, pl.ds(first_group, count)],
                    dst_ref=rtracks.at[h, me, pl.ds(first_group, count)],
                    send_sem=send2_sem,
                    recv_sem=recv2_sem.at[h + c],
                    device_id=(chan, there),
                    device_id_type=MESH,
                ).start()

    def folds(h, c, first_group, count):
        def fold(step, carry):
            q = step // STEPS
            s = step % STEPS
            left = []
            for e in range(WIDE):
                series = rtracks[h, s * WIDE + e, q]
                low_now = low[h, q, :, pl.ds(pl.multiple_of((s * WIDE + e) * TD, TD), TD)]
                left.append(
                    jnp.concatenate(
                        [jnp.where(low_now == v, series, zero) for v in range(16)], axis=0
                    )
                )
            span = pl.ds(pl.multiple_of(s * WIDE * TD, WIDE * TD), WIDE * TD)
            grid[q] += jnp.dot(
                jnp.concatenate(left, axis=1), right[h, q, span, :], preferred_element_type=F32
            )
            return carry

        span = rtracks.at[h, pl.ds(0, BLK - 1), pl.ds(first_group, count)]
        pltpu.make_async_copy(span, span, recv2_sem.at[h + c]).wait()
        lax.fori_loop(first_group * STEPS, (first_group + count) * STEPS, fold, 0)

    sections(0)
    forms(0)
    picks(0)
    sections(1, HOLD, lambda: send_tracks(0))
    forms(1)
    picks(1)
    send_tracks(1)

    for g in range(2):
        both = [acc[h, g].T.reshape(16, SUMS, TD) for h in range(2)]
        inten[pl.ds(16 * g, 16)] = jnp.concatenate(both, axis=1).astype(BF16)
    rinten[me] = inten[me]
    for route in routes():
        there = towards(route)
        pltpu.make_async_remote_copy(
            src_ref=inten.at[there],
            dst_ref=rinten.at[me],
            send_sem=send3_sem,
            recv_sem=recv3_sem,
            device_id=(chan, there),
            device_id_type=MESH,
        ).start()

    same = (
        lax.broadcasted_iota(jnp.int32, (256, 256), 0) % 16
        == lax.broadcasted_iota(jnp.int32, (256, 256), 1) % 16
    )
    lane = lax.broadcasted_iota(jnp.int32, (1, 1, 1, 256), 3)
    sub = lax.broadcasted_iota(jnp.int32, (2, 8, 256), 1)

    def profile(first_group, count):
        level = grid[pl.ds(first_group, count)]
        level = jnp.where(same, level, 0.0).reshape(count, 32, 8, 256)
        for d in (8, 4, 2, 1):
            upper = (lane // d) % 2 == 1
            lower_part, upper_part = level[:, : 2 * d], level[:, 2 * d :]
            stay = jnp.where(upper, upper_part, lower_part)
            flat = jnp.where(upper, lower_part, upper_part).reshape(count * 2 * d * 8, 256)
            down = pltpu.roll(flat, d, 1).reshape(count, 2 * d, 8, 256)
            up = pltpu.roll(flat, 256 - d, 1).reshape(count, 2 * d, 8, 256)
            level = stay + jnp.where(upper, down, up)
        found = jnp.zeros((2, 8, 256), F32)
        for q in range(count):
            sums = level[q] + pltpu.roll(level[q], 6, 1)
            sums = sums + pltpu.roll(sums, 7, 1)
            sums = jnp.where(sub % 4 == 0, sums, 0.0)
            found = found + (pltpu.roll(sums, first_group + q, 1) if first_group + q else sums)
        return found

    folds(0, 0, 0, 4)
    total = jnp.zeros((2, 8, 256), F32)
    for c, (first_group, count) in enumerate(CHUNKS[1]):
        folds(1, c, first_group, count)
        total = total + profile(first_group, count)
    part[...] = total.reshape(PSR, NBIN) * (NBIN / (4 * CHD * float(TIME)))
    for dy in (2, 1, 3):
        pltpu.make_async_remote_copy(
            src_ref=part,
            dst_ref=parts.at[dy - 1],
            send_sem=send4_sem,
            recv_sem=recv4_sem.at[dy - 1],
            device_id=((chan + dy) % 4, me),
            device_id_type=MESH,
        ).start()

    span = rinten.at[pl.ds(0, BLK - 1)]
    pltpu.make_async_copy(span, span, recv3_sem).wait()
    averages = rinten[...].astype(F32)
    sides = [
        averages[:, h * SUMS : (h + 1) * SUMS].reshape(256, TD).T.reshape(16, 8, 256)
        for h in range(2)
    ]
    even, odd = halves(*sides)
    inten_out[...] = jnp.stack([even, odd], axis=1).reshape(BLK, CHD, 256)
    for dy in range(1, 4):
        pltpu.make_async_copy(part, parts.at[dy - 1], recv4_sem.at[dy - 1]).wait()
    folded_out[...] = part[...] + parts[0] + parts[1] + parts[2]

    span = recv.at[:, pl.ds(0, BLK - 1)]
    pltpu.make_async_copy(span, span, send_sem).wait()
    span = rtracks.at[:, pl.ds(0, BLK - 1)]
    pltpu.make_async_copy(span, span, send2_sem).wait()
    span = rinten.at[pl.ds(0, BLK - 1)]
    pltpu.make_async_copy(span, span, send3_sem).wait()
    pltpu.make_async_copy(parts, parts, send4_sem).wait()


def shards(volt, pulsar_beam, phase_bin):
    first, second, turns, avg = tables()
    far = pl.BlockSpec(memory_space=pltpu.HBM)
    whole = pl.BlockSpec(memory_space=pltpu.VMEM)
    dma = pltpu.SemaphoreType.DMA
    return pl.pallas_call(
        kernel,
        out_shape=(
            jax.ShapeDtypeStruct((BLK, CHD, TIME // DS), F32),
            jax.ShapeDtypeStruct((PSR, NBIN), F32),
        ),
        in_specs=[far] * 7,
        out_specs=(whole, whole),
        scratch_shapes=[
            pltpu.VMEM((2, PAIRS, 16, TIME), BF16),
            pltpu.VMEM((2, BLK, PAIRS, 16, TD), BF16),
            pltpu.VMEM((2, BLK, PAIRS, 16, TD), BF16),
            pltpu.VMEM((BLK, PAIRS, 16, TD), BF16),
            pltpu.VMEM((8 + 4 * F + 8, TD), F32),
            pltpu.VMEM((2, BLK, NQ, 16, TD), BF16),
            pltpu.VMEM((2, BLK, NQ, 16, TD), BF16),
            pltpu.VMEM((BLK, 2 * SUMS, TD), BF16),
            pltpu.VMEM((BLK, 2 * SUMS, TD), BF16),
            pltpu.VMEM((2, 2, TD, TD), F32),
            pltpu.VMEM((PSR, CHD, TIME), jnp.int32),
            pltpu.VMEM((2, NQ, 16, TIME), BF16),
            pltpu.VMEM((2, NQ, TIME, 256), BF16),
            pltpu.VMEM((NQ, 256, 256), F32),
            pltpu.VMEM((PSR, NBIN), F32),
            pltpu.VMEM((3, PSR, NBIN), F32),
            pltpu.VMEM((512, 512), BF16),
            pltpu.VMEM((256, 256), BF16),
            pltpu.VMEM((4, BLK, 8, TD), F32),
            pltpu.VMEM((4, 4 * TD, TD), BF16),
            pltpu.VMEM((2, BLK, 8, TD), F32),
            pltpu.SMEM((512,), jnp.int32),
            dma((7,)),
            dma((CUT,)),
            dma(()),
            dma((2 * CUT,)),
            dma(()),
            dma((4,)),
            dma(()),
            dma(()),
            dma(()),
            dma((3,)),
        ],
        compiler_params=pltpu.CompilerParams(
            collective_id=0, has_side_effects=True, vmem_limit_bytes=50 * 1024 * 1024
        ),
        name="beams",
    )(
        *(
            pltpu.with_memory_space_constraint(operand, pltpu.HBM)
            for operand in (
                volt.reshape(2, PAIRS, 16, TIME),
                pulsar_beam,
                phase_bin,
                jnp.asarray(first),
                jnp.asarray(second),
                jnp.asarray(turns),
                jnp.asarray(avg),
            )
        )
    )


def solution(mesh):
    placed = (P(None, "feed", "chan", None), P(), P("feed", None, None))
    return jax.shard_map(
        shards,
        mesh=mesh,
        in_specs=placed,
        out_specs=(P("feed", "chan", None), P("feed", None)),
        check_vma=False,
    )
```

```python
import math

import jax
import jax.numpy as jnp
import ml_dtypes
import numpy as np
from jax import lax
from jax.experimental import pallas as pl
from jax.experimental.pallas import tpu as pltpu
from jax.sharding import PartitionSpec as P

F = 1024
NBIN = 256
DS = 16
TIME = 4096
BLK = 32
CHD = 8
TD = 128
PSR = 16
NQ = 4
PAIRS = 16
PIECES = (((0, 2), (2, 2), (4, 4), (8, 4), (12, 4)), ((0, 4), (4, 4), (8, 4), (12, 2), (14, 2)))
CUT = 5
HOLD = 4
WIDE = 16
STEPS = BLK // WIDE
CHUNKS = (((0, 4),), ((0, 2), (2, 1), (3, 1)))
SUMS = TD // DS
MESH = pl.DeviceIdType.MESH
F32 = jnp.float32
BF16 = jnp.bfloat16


def reverse_bits(number, bit_count):
    return sum((number >> b & 1) << bit_count - 1 - b for b in range(bit_count))


def tables():
    idx = np.arange(BLK)
    rev = np.array([reverse_bits(i, 5) for i in range(BLK)])

    def transform(out_idx):
        angle = 2.0 * math.pi * (np.outer(out_idx, idx) % BLK) / BLK
        cos, sin = np.cos(angle), np.sin(angle)
        return np.array([[cos, sin], [-sin, cos]])

    first = np.einsum("aboi,cd->aocibd", transform(rev), np.eye(8)).reshape(512, 512)
    within = transform(idx).reshape(2, 2, BLK, PAIRS, 2)
    second = np.einsum("aboij,cd->aocibjd", within, np.eye(4)).reshape(256, 256)
    step = np.exp(-2j * math.pi * 2 * rev / F)[:, None] * np.ones((1, 8))
    start = np.exp(-2j * math.pi * np.outer(rev, np.arange(8) // 4) / F) / 32.0
    turns = np.stack([step.real, step.imag, start.real, start.imag])
    turns = turns[..., None] * np.ones(TD)
    avg = np.zeros((4, 4, TD, 16, SUMS))
    for j in range(4):
        for b in range(4):
            for t in range(TD):
                avg[j, b, t, 4 * j + b, t // DS] = 1.0 / DS
    avg = avg.reshape(4, 4 * TD, TD)
    bf = ml_dtypes.bfloat16
    return first.astype(bf), second.astype(bf), turns.astype(np.float32), avg.astype(bf)


def routes():
    rings = (
        ((2, 2),),
        ((1, 2), (2, 1), (3, 2), (2, 3)),
        ((1, 1), (3, 1), (3, 3), (1, 3)),
        ((2, 0), (0, 2)),
        ((1, 0), (0, 1), (3, 0), (0, 3)),
        ((0, 0),),
    )
    found = [(dz, dx, dc) for ring in rings for dc in (0, 1) for dz, dx in ring]
    return [route for route in found if route != (0, 0, 0)]


def halves(low_rows, high_rows):
    upper = lax.broadcasted_iota(jnp.int32, low_rows.shape, low_rows.ndim - 2) >= 4
    axis = low_rows.ndim - 2
    return (
        jnp.where(upper, pltpu.roll(high_rows, 4, axis), low_rows),
        jnp.where(upper, high_rows, pltpu.roll(low_rows, 4, axis)),
    )


def kernel(
    volt,
    beam_in,
    phase,
    first_in,
    second_in,
    turns_in,
    avg_in,
    inten_out,
    folded_out,
    held,
    sent,
    recv,
    mid,
    det,
    tracks,
    rtracks,
    inten,
    rinten,
    acc,
    bins,
    low,
    right,
    grid,
    part,
    parts,
    first,
    second,
    turns,
    avg,
    turn,
    beam,
    local_sem,
    held_sem,
    send_sem,
    recv_sem,
    send2_sem,
    recv2_sem,
    send3_sem,
    recv3_sem,
    send4_sem,
    recv4_sem,
):
    me = lax.axis_index("feed")
    chan = lax.axis_index("chan")
    core = me % 2
    x = me // 2 % 4
    z = me // 8

    def towards(route):
        dz, dx, dc = route
        return (((z + dz) % 4) * 4 + (x + dx) % 4) * 2 + (core + dc) % 2

    reads = []
    for c, piece in enumerate(PIECES[0]):
        span = pl.ds(*piece)
        reads.append(pltpu.make_async_copy(volt.at[:, span], held.at[:, span], held_sem.at[c]))
        reads[-1].start()
    barrier = pltpu.get_barrier_semaphore()
    for route in routes():
        pl.semaphore_signal(
            barrier, inc=1, device_id=(chan, towards(route)), device_id_type=MESH
        )
    for dy in range(1, 4):
        pl.semaphore_signal(
            barrier, inc=1, device_id=((chan + dy) % 4, me), device_id_type=MESH
        )
    loads = [
        pltpu.make_async_copy(first_in, first, local_sem.at[0]),
        pltpu.make_async_copy(turns_in, turns, local_sem.at[1]),
        pltpu.make_async_copy(
            phase.at[:, pl.ds(pl.multiple_of(chan * CHD, CHD), CHD), :], bins, local_sem.at[2]
        ),
        pltpu.make_async_copy(second_in, second, local_sem.at[3]),
        pltpu.make_async_copy(avg_in, avg, local_sem.at[4]),
        pltpu.make_async_copy(beam_in, beam, local_sem.at[5]),
    ]
    for load in loads:
        load.start()

    def arrange(i, carry):
        real = held[0, i].astype(F32)
        imag = held[1, i].astype(F32)
        real0, real1 = halves(real[:8], real[8:])
        imag0, imag1 = halves(imag[:8], imag[8:])
        for h, tile in enumerate(((real0, imag0), (real1, imag1))):
            tile = jnp.concatenate(tile, axis=0).astype(BF16)
            for d in range(BLK):
                sent[h, d, i] = tile[:, d * TD : (d + 1) * TD]
        return carry

    def send(h, c, first_pair, count):
        for route in routes():
            there = towards(route)
            pltpu.make_async_remote_copy(
                src_ref=sent.at[h, there, pl.ds(first_pair, count)],
                dst_ref=recv.at[h, me, pl.ds(first_pair, count)],
                send_sem=send_sem,
                recv_sem=recv_sem.at[h * CUT + c],
                device_id=(chan, there),
                device_id_type=MESH,
            ).start()

    for c, (first_pair, count) in enumerate(PIECES[0]):
        reads[c].wait()
        lax.fori_loop(first_pair, first_pair + count, arrange, 0)
        if c == 0:
            pl.semaphore_wait(barrier, 34)
        send(0, c, first_pair, count)
    own = pltpu.make_async_copy(sent.at[:, me], recv.at[:, me], local_sem.at[6])
    own.start()

    def send_later(c, carry):
        send(1, c, c * 4, 4)
        return carry

    lax.fori_loop(0, 3, send_later, 0)
    send(1, 3, 12, 2)
    send(1, 4, 14, 2)

    zero = jnp.zeros((16, TD), BF16)
    one = jnp.ones((16, TD), BF16)
    loads[2].wait()

    def digits(step, carry):
        q = step // 4
        span = pl.ds(pl.multiple_of(step % 4 * 8 * TD, 8 * TD), 8 * TD)
        top0, top1 = halves(bins[q, :, span], bins[q + 4, :, span])
        bottom0, bottom1 = halves(bins[q + 8, :, span], bins[q + 12, :, span])
        for h, tile in enumerate(((top0, bottom0), (top1, bottom1))):
            tile = jnp.concatenate(tile, axis=0)
            low[h, q, :, span] = (tile & 15).astype(F32).astype(BF16)
            high = (tile >> 4).astype(F32).astype(BF16)
            marks = [
                jnp.concatenate(
                    [
                        jnp.where(high[:, e * TD : (e + 1) * TD] == v, one, zero)
                        for v in range(16)
                    ],
                    axis=0,
                )
                for e in range(8)
            ]
            right[h, q, span, :] = jnp.concatenate(marks, axis=1).T
        return carry

    lax.fori_loop(0, 4 * NQ, digits, 0)
    acc[...] = jnp.zeros_like(acc)
    grid[...] = jnp.zeros_like(grid)
    for load in loads[:2] + loads[3:]:
        load.wait()
    own.wait()

    def sections(h, before=None, then=None):
        turn[...] = turns[2:]

        def section(i, carry):
            operand = jnp.concatenate(
                [recv[h, :, 2 * i + e].reshape(512, TD) for e in range(2)], axis=1
            )
            result = jnp.dot(first[...], operand, preferred_element_type=F32)
            for e in range(2):
                value = result[:, e * TD : (e + 1) * TD].reshape(2, BLK, 8, TD)
                tr, ti = turn[0], turn[1]
                turned = (value[0] * tr - value[1] * ti, value[0] * ti + value[1] * tr)
                mid[:, 2 * i + e] = jnp.concatenate(turned, axis=1).astype(BF16)
                sr, si = turns[0], turns[1]
                turn[0] = tr * sr - ti * si
                turn[1] = tr * si + ti * sr
            return carry

        for c, (first_pair, count) in enumerate(PIECES[h]):
            if c == before:
                then()
            span = recv.at[h, pl.ds(0, BLK - 1), pl.ds(first_pair, count)]
            pltpu.make_async_copy(span, span, recv_sem.at[h * CUT + c]).wait()
            lax.fori_loop(first_pair // 2, (first_pair + count) // 2, section, 0)

    def forms(h):
        def form(j, carry):
            operand = jnp.concatenate(
                [mid[4 * j + b].reshape(256, TD) for b in range(4)], axis=1
            )
            result = jnp.dot(second[...], operand, preferred_element_type=F32)
            power = result[:128] * result[:128] + result[128:] * result[128:]
            for b in range(4):
                place = pl.multiple_of(8 + (4 * j + b) * 128, 8)
                det[pl.ds(place, 128), :] = power[:, b * TD : (b + 1) * TD]
            acc[h, j // 4] += jnp.dot(power.astype(BF16), avg[j % 4], preferred_element_type=F32)
            return carry

        lax.fori_loop(0, BLK // 4, form, 0, unroll=2)

    upper_rows = lax.broadcasted_iota(jnp.int32, (8, TD), 0) >= 4

    def picks(h):
        def pick(d, carry):
            for q in range(NQ):
                found = []
                for n in range(4):
                    row = beam[d * PSR + 4 * n + q]
                    found.append(det[pl.ds(8 + 4 * row - 4 * (n % 2), 8), :])
                tile = [jnp.where(upper_rows, found[n + 1], found[n]) for n in (0, 2)]
                tracks[h, d, q] = jnp.concatenate(tile, axis=0).astype(BF16)
            return carry

        lax.fori_loop(0, BLK, pick, 0, unroll=4)
        rtracks[h, me] = tracks[h, me]

    def send_tracks(h):
        for c, (first_group, count) in enumerate(CHUNKS[h]):
            for route in routes():
                there = towards(route)
                pltpu.make_async_remote_copy(
                    src_ref=tracks.at[h, there, pl.ds(first_group, count)],
                    dst_ref=rtracks.at[h, me, pl.ds(first_group, count)],
                    send_sem=send2_sem,
                    recv_sem=recv2_sem.at[h + c],
                    device_id=(chan, there),
                    device_id_type=MESH,
                ).start()

    def folds(h, c, first_group, count):
        def fold(step, carry):
            q = step // STEPS
            s = step % STEPS
            left = []
            for e in range(WIDE):
                series = rtracks[h, s * WIDE + e, q]
                low_now = low[h, q, :, pl.ds(pl.multiple_of((s * WIDE + e) * TD, TD), TD)]
                left.append(
                    jnp.concatenate(
                        [jnp.where(low_now == v, series, zero) for v in range(16)], axis=0
                    )
                )
            span = pl.ds(pl.multiple_of(s * WIDE * TD, WIDE * TD), WIDE * TD)
            grid[q] += jnp.dot(
                jnp.concatenate(left, axis=1), right[h, q, span, :], preferred_element_type=F32
            )
            return carry

        span = rtracks.at[h, pl.ds(0, BLK - 1), pl.ds(first_group, count)]
        pltpu.make_async_copy(span, span, recv2_sem.at[h + c]).wait()
        lax.fori_loop(first_group * STEPS, (first_group + count) * STEPS, fold, 0)

    sections(0)
    forms(0)
    picks(0)
    sections(1, HOLD, lambda: send_tracks(0))
    forms(1)
    picks(1)
    send_tracks(1)

    for g in range(2):
        both = [acc[h, g].T.reshape(16, SUMS, TD) for h in range(2)]
        inten[pl.ds(16 * g, 16)] = jnp.concatenate(both, axis=1).astype(BF16)
    rinten[me] = inten[me]
    for route in routes():
        there = towards(route)
        pltpu.make_async_remote_copy(
            src_ref=inten.at[there],
            dst_ref=rinten.at[me],
            send_sem=send3_sem,
            recv_sem=recv3_sem,
            device_id=(chan, there),
            device_id_type=MESH,
        ).start()

    same = (
        lax.broadcasted_iota(jnp.int32, (256, 256), 0) % 16
        == lax.broadcasted_iota(jnp.int32, (256, 256), 1) % 16
    )
    lane = lax.broadcasted_iota(jnp.int32, (1, 1, 1, 256), 3)
    sub = lax.broadcasted_iota(jnp.int32, (2, 8, 256), 1)

    def profile(first_group, count):
        level = grid[pl.ds(first_group, count)]
        level = jnp.where(same, level, 0.0).reshape(count, 32, 8, 256)
        for d in (8, 4, 2, 1):
            upper = (lane // d) % 2 == 1
            lower_part, upper_part = level[:, : 2 * d], level[:, 2 * d :]
            stay = jnp.where(upper, upper_part, lower_part)
            flat = jnp.where(upper, lower_part, upper_part).reshape(count * 2 * d * 8, 256)
            down = pltpu.roll(flat, d, 1).reshape(count, 2 * d, 8, 256)
            up = pltpu.roll(flat, 256 - d, 1).reshape(count, 2 * d, 8, 256)
            level = stay + jnp.where(upper, down, up)
        found = jnp.zeros((2, 8, 256), F32)
        for q in range(count):
            sums = level[q] + pltpu.roll(level[q], 6, 1)
            sums = sums + pltpu.roll(sums, 7, 1)
            sums = jnp.where(sub % 4 == 0, sums, 0.0)
            found = found + (pltpu.roll(sums, first_group + q, 1) if first_group + q else sums)
        return found

    folds(0, 0, 0, 4)
    total = jnp.zeros((2, 8, 256), F32)
    for c, (first_group, count) in enumerate(CHUNKS[1]):
        folds(1, c, first_group, count)
        total = total + profile(first_group, count)
    part[...] = total.reshape(PSR, NBIN) * (NBIN / (4 * CHD * float(TIME)))
    for dy in (2, 1, 3):
        pltpu.make_async_remote_copy(
            src_ref=part,
            dst_ref=parts.at[dy - 1],
            send_sem=send4_sem,
            recv_sem=recv4_sem.at[dy - 1],
            device_id=((chan + dy) % 4, me),
            device_id_type=MESH,
        ).start()

    span = rinten.at[pl.ds(0, BLK - 1)]
    pltpu.make_async_copy(span, span, recv3_sem).wait()
    averages = rinten[...].astype(F32)
    sides = [
        averages[:, h * SUMS : (h + 1) * SUMS].reshape(256, TD).T.reshape(16, 8, 256)
        for h in range(2)
    ]
    even, odd = halves(*sides)
    inten_out[...] = jnp.stack([even, odd], axis=1).reshape(BLK, CHD, 256)
    for dy in range(1, 4):
        pltpu.make_async_copy(part, parts.at[dy - 1], recv4_sem.at[dy - 1]).wait()
    folded_out[...] = part[...] + parts[0] + parts[1] + parts[2]

    span = recv.at[:, pl.ds(0, BLK - 1)]
    pltpu.make_async_copy(span, span, send_sem).wait()
    span = rtracks.at[:, pl.ds(0, BLK - 1)]
    pltpu.make_async_copy(span, span, send2_sem).wait()
    span = rinten.at[pl.ds(0, BLK - 1)]
    pltpu.make_async_copy(span, span, send3_sem).wait()
    pltpu.make_async_copy(parts, parts, send4_sem).wait()


def shards(volt, pulsar_beam, phase_bin):
    first, second, turns, avg = tables()
    far = pl.BlockSpec(memory_space=pltpu.HBM)
    whole = pl.BlockSpec(memory_space=pltpu.VMEM)
    dma = pltpu.SemaphoreType.DMA
    return pl.pallas_call(
        kernel,
        out_shape=(
            jax.ShapeDtypeStruct((BLK, CHD, TIME // DS), F32),
            jax.ShapeDtypeStruct((PSR, NBIN), F32),
        ),
        in_specs=[far] * 7,
        out_specs=(whole, whole),
        scratch_shapes=[
            pltpu.VMEM((2, PAIRS, 16, TIME), BF16),
            pltpu.VMEM((2, BLK, PAIRS, 16, TD), BF16),
            pltpu.VMEM((2, BLK, PAIRS, 16, TD), BF16),
            pltpu.VMEM((BLK, PAIRS, 16, TD), BF16),
            pltpu.VMEM((8 + 4 * F + 8, TD), F32),
            pltpu.VMEM((2, BLK, NQ, 16, TD), BF16),
            pltpu.VMEM((2, BLK, NQ, 16, TD), BF16),
            pltpu.VMEM((BLK, 2 * SUMS, TD), BF16),
            pltpu.VMEM((BLK, 2 * SUMS, TD), BF16),
            pltpu.VMEM((2, 2, TD, TD), F32),
            pltpu.VMEM((PSR, CHD, TIME), jnp.int32),
            pltpu.VMEM((2, NQ, 16, TIME), BF16),
            pltpu.VMEM((2, NQ, TIME, 256), BF16),
            pltpu.VMEM((NQ, 256, 256), F32),
            pltpu.VMEM((PSR, NBIN), F32),
            pltpu.VMEM((3, PSR, NBIN), F32),
            pltpu.VMEM((512, 512), BF16),
            pltpu.VMEM((256, 256), BF16),
            pltpu.VMEM((4, BLK, 8, TD), F32),
            pltpu.VMEM((4, 4 * TD, TD), BF16),
            pltpu.VMEM((2, BLK, 8, TD), F32),
            pltpu.SMEM((512,), jnp.int32),
            dma((7,)),
            dma((CUT,)),
            dma(()),
            dma((2 * CUT,)),
            dma(()),
            dma((4,)),
            dma(()),
            dma(()),
            dma(()),
            dma((3,)),
        ],
        compiler_params=pltpu.CompilerParams(
            collective_id=0, has_side_effects=True, vmem_limit_bytes=50 * 1024 * 1024
        ),
        name="beams",
    )(
        *(
            pltpu.with_memory_space_constraint(operand, pltpu.HBM)
            for operand in (
                volt.reshape(2, PAIRS, 16, TIME),
                pulsar_beam,
                phase_bin,
                jnp.asarray(first),
                jnp.asarray(second),
                jnp.asarray(turns),
                jnp.asarray(avg),
            )
        )
    )


def solution(mesh):
    placed = (P(None, "feed", "chan", None), P(), P("feed", None, None))
    return jax.shard_map(
        shards,
        mesh=mesh,
        in_specs=placed,
        out_specs=(P("feed", "chan", None), P("feed", None)),
        check_vma=False,
    )
```
